32 devices in a mesh: groups: 2 (over x), gx: 16 (over z, y, core).
Axes of the slice: x: 2, y: 2, z: 4, core: 2. Of those that a mesh axis runs over, the one named last changes fastest.
Arguments:
- volume: bfloat16 [32, 256, 6, 128], P('groups', 'gx'), parts along dimension 0, may hold values from -6 to 6
- conv_weight: bfloat16 [256, 27, 128], P('gx'), may hold values from -0.078125 to 0.078125
- conv_bias: float32 [128], replicated, may hold values from -3 to 3
- tconv_weight: bfloat16 [27, 64, 128], replicated, may hold values from -0.25 to 0.25
Outputs:
- decoded: bfloat16 [64, 64, 12, 256], P(('groups', 'gx')), parts along dimension 0
The draws below stay inside these ranges and needn't reach their ends.
There are 2 independent parts, one for each index of `groups`. The reference program is written for one: setup_inputs(seed, part) draws one part's arguments, and reference() takes and returns one part's arrays. A program takes and returns all parts, laid end to end along the dimension named above; an argument that names none is the same for every part. Nothing has to cross between parts.
All inputs are finite; a program needn't handle non-finite values.
Results may differ from the reference program's by a relative error of at most 0.005.
Values may be sent and summed in bfloat16 or wider, within the bound.
No kernel may reach another device: no remote copies, remote signals or barrier semaphores. Data moves between devices by JAX's collectives and lax.ppermute only.
A program may use at most 64 MiB of HBM per device.

```python
import jax
import jax.numpy as jnp
from jax import lax

CIN = 256
COUT = 128
CUP = 64
WY = 6
WZ = 128
NX = 16


def raised(values, stream_key, source, target, blocks, factor):
    def block_of(axis_at):
        return (jnp.arange(values.shape[axis_at]) // (values.shape[axis_at] // blocks)).reshape((-1,) + (1,) * (values.ndim - 1 - axis_at))

    one_side = jax.random.permutation(stream_key, blocks)[block_of(target)]
    second = (block_of(target) + blocks // 2) % blocks
    return jnp.where((block_of(source) == one_side) | (block_of(source) == second), factor * values, values)


def block_scale(key, shape, shards, smallest, top_value):
    loudness = 1.0
    for axis_at, shards_of in shards:
        draws = jax.random.uniform(jax.random.fold_in(jax.random.fold_in(key, 6), axis_at), (shards_of,), jnp.float32, smallest / len(shards), top_value / len(shards))
        loudness = loudness * jnp.repeat(jnp.exp(draws), shape[axis_at] // shards_of).reshape((-1,) + (1,) * (len(shape) - 1 - axis_at))
    return loudness


def bell_draw(own_key, extent, width, reach, cuts=(), kind=jnp.bfloat16):
    factor_of = block_scale(own_key, extent, cuts, -0.22, 0.18) if cuts else 1.0
    values = jax.random.normal(own_key, extent, jnp.float32) * width * factor_of
    return jnp.minimum(jnp.maximum(values, -reach), reach).astype(kind)


def bell_draw_with(rng, dims, deviation, reach, shards, heavy, kind=jnp.bfloat16):
    entries = deviation * jax.random.normal(rng, dims, jnp.float32)
    if shards:
        entries = entries * block_scale(rng, dims, shards, -0.22, 0.18)
    return jnp.clip(raised(entries, jax.random.fold_in(rng, 3), *heavy), -reach, reach).astype(kind)


def setup_inputs(seed: int = 0, part: int = 0) -> dict:
    arg_keys = jax.random.split(jax.random.key(seed), 5)
    part_splits = jax.random.split(jax.random.fold_in(arg_keys[4], part), 5)
    volume = bell_draw_with(part_splits[0], (NX, CIN, WY, WZ), 1.0, 6.0, ((1, 16),), (1, 0, 16, 2.0))
    conv_weight = bell_draw(arg_keys[1], (CIN, 27, COUT), (CIN * 27) ** -0.5, 0.078125, ((0, 16),))
    conv_bias = bell_draw(arg_keys[2], (COUT,), 0.5, 3.0, (), jnp.float32)
    tconv_weight = bell_draw(arg_keys[3], (27, CUP, COUT), (COUT * 4) ** -0.5, 0.25)
    return {"volume": volume, "conv_weight": conv_weight, "conv_bias": conv_bias, "tconv_weight": tconv_weight}


def next_cell(field, axis):
    size = field.shape[axis]
    rest = lax.slice_in_dim(field, 1, size, axis=axis)
    zero_shape = list(field.shape)
    zero_shape[axis] = 1
    return jnp.concatenate([rest, jnp.zeros(zero_shape, field.dtype)], axis=axis)


def yz_classes(products, tap_x):
    layout_options = (((1, False),), ((2, False), (0, True)))
    parity_classes = []
    for par_y in range(2):
        for par_z in range(2):
            total = jnp.zeros(products.shape[:1] + products.shape[4:], jnp.float32)
            for tap_y, shift_y in layout_options[par_y]:
                for tap_z, shift_z in layout_options[par_z]:
                    term = products[:, tap_x, tap_y, tap_z]
                    if shift_y:
                        term = next_cell(term, 2)
                    if shift_z:
                        term = next_cell(term, 3)
                    total = total + term
            parity_classes.append(total)
    return jnp.stack(parity_classes, axis=0)


def alternate(even, odd):
    both = jnp.stack([even, odd], axis=0)
    rows, chans, wide_y, wide_z = both.shape[2], both.shape[3], both.shape[4], both.shape[5]
    both = both.reshape(2, 2, 2, rows, chans, wide_y, wide_z)
    both = jnp.transpose(both, (3, 0, 4, 5, 1, 6, 2))
    return both.reshape(2 * rows, chans, 2 * wide_y, 2 * wide_z)


def reference(volume, conv_weight, conv_bias, tconv_weight):
    cin, cout = conv_weight.shape[0], conv_weight.shape[2]
    kernel = conv_weight.reshape(cin, 3, 3, 3, cout)
    kernel = jnp.transpose(kernel, (4, 0, 1, 2, 3))
    lhs = jnp.transpose(volume, (1, 0, 2, 3))[None]
    conv = lax.conv_general_dilated(lhs, kernel, (1, 1, 1), [(1, 1), (1, 1), (1, 1)],
                                    dimension_numbers=("NCDHW", "OIDHW", "NCDHW"),
                                    preferred_element_type=jnp.float32)
    conv = jnp.transpose(conv[0], (1, 0, 2, 3))
    hidden = jnp.maximum(conv + conv_bias[None, :, None, None], 0.0).astype(jnp.bfloat16)
    cup = tconv_weight.shape[1]
    rows, wide_y, wide_z = hidden.shape[0], hidden.shape[2], hidden.shape[3]
    flattened_patches = tconv_weight.reshape(27 * cup, cout).astype(jnp.float32)
    products = jnp.einsum("oc,xcyz->xoyz", flattened_patches, hidden.astype(jnp.float32))
    products = products.reshape(rows, 3, 3, 3, cup, wide_y, wide_z)
    first = yz_classes(products, 0)
    middle = yz_classes(products, 1)
    last = yz_classes(products, 2)
    odd = last + next_cell(first, 1)
    return alternate(middle, odd).astype(jnp.bfloat16)
```

```python
import functools

import jax
import jax.numpy as jnp
from jax import lax
from jax.experimental import pallas as pl
from jax.experimental.pallas import tpu as pltpu
from jax.sharding import PartitionSpec as P

TILE = 4


def window(first, count, total):
    return jnp.clip(first, 0, total - count)


def body(parts, total, scalars, *refs):
    vols, weights = refs[:parts], refs[parts : 2 * parts]
    bias_ref, up_ref, out_ref, cells, taps, upper = refs[2 * parts :]
    slots, cin = cells.shape[0], cells.shape[2]
    wide_y, wide_z = cells.shape[1] - 2, cells.shape[3]
    cout = taps.shape[1] // 3
    cup = up_ref.shape[1]
    plane = scalars[0]
    blank = jnp.zeros((slots, cin, wide_z), cells.dtype)
    cells[:, 0] = blank
    cells[:, wide_y + 1] = blank
    row = 0
    for part in range(parts):
        vol, weight = vols[part], weights[part]
        chans = vol.shape[2]
        for slot in range(slots):
            at = plane - 1 + slot
            inside = jnp.logical_and(at >= 0, at < total)
            held = vol[jnp.clip(at - scalars[1 + part], 0, vol.shape[0] - 1)]
            cells[slot, 1 : wide_y + 1, row : row + chans] = jnp.where(inside, held, jnp.zeros_like(held))
        row += chans
    for tap in range(27):
        column = jnp.concatenate([weight[tap] for weight in weights], axis=0)
        at = tap % 3 * cout
        taps[tap // 3, at : at + cout] = column.T
    eye = lax.broadcasted_iota(jnp.int32, (cout, cout), 0) == lax.broadcasted_iota(jnp.int32, (cout, cout), 1)
    bias = jnp.sum(jnp.where(eye, bias_ref[...], 0.0), axis=1, keepdims=True)
    lane = lax.broadcasted_iota(jnp.int32, (cout, wide_z), 1)
    hidden = []
    for ahead in range(2):
        rows = []
        for pair in range(wide_y // 2):
            acc = jnp.zeros((3 * cout, 2 * wide_z), jnp.float32)
            for tap_x in range(3):
                for tap_y in range(3):
                    at = 2 * pair + tap_y
                    block = jnp.concatenate([cells[ahead + tap_x, at], cells[ahead + tap_x, at + 1]], axis=1)
                    acc += jnp.dot(taps[3 * tap_x + tap_y], block, preferred_element_type=jnp.float32)
            for side in range(2):
                cut = acc[:, side * wide_z : (side + 1) * wide_z]
                low = jnp.where(lane == 0, 0.0, pltpu.roll(cut[:cout], 1, 1))
                high = jnp.where(lane == wide_z - 1, 0.0, pltpu.roll(cut[2 * cout :], wide_z - 1, 1))
                summed = cut[cout : 2 * cout] + low + high
                value = jnp.maximum(summed + bias, 0.0)
                if ahead:
                    value = jnp.where(plane + 1 < total, value, 0.0)
                rows.append(value.astype(jnp.bfloat16))
        hidden.append(jnp.concatenate(rows, axis=1))
    upper[:cout] = hidden[0]
    upper[cout:] = hidden[1]
    shape = (2 * wide_z, 2 * wide_z)
    source, target = (lax.broadcasted_iota(jnp.int32, shape, axis) for axis in range(2))
    weave = (target == 2 * (source % wide_z) + source // wide_z).astype(jnp.bfloat16)
    edge = lax.broadcasted_iota(jnp.int32, (cup, wide_z), 1) == wide_z - 1

    def later(value):
        return jnp.where(edge, 0.0, pltpu.roll(value, wide_z - 1, 1))

    for odd in range(2):
        if odd:
            left = jnp.concatenate([up_ref[18:27].reshape(9 * cup, cout), up_ref[0:9].reshape(9 * cup, cout)], axis=1)
            right = upper[...]
        else:
            left = up_ref[9:18].reshape(9 * cup, cout)
            right = upper[:cout]
        product = jnp.dot(left, right, preferred_element_type=jnp.float32)

        def term(tap_y, tap_z, y):
            at = (3 * tap_y + tap_z) * cup
            return product[at : at + cup, y * wide_z : (y + 1) * wide_z]

        lines = []
        for y in range(wide_y):
            for par_y in range(2):
                choices = [(1, y)] if par_y == 0 else [(2, y)] + ([(0, y + 1)] if y + 1 < wide_y else [])
                even = sum(term(tap_y, 1, at) for tap_y, at in choices)
                plain = sum(term(tap_y, 2, at) for tap_y, at in choices)
                moved = sum(term(tap_y, 0, at) for tap_y, at in choices)
                lines.append(jnp.concatenate([even, plain + later(moved)], axis=1).astype(jnp.bfloat16))
        woven = jnp.dot(jnp.concatenate(lines, axis=0), weave, preferred_element_type=jnp.float32)
        out_ref[odd] = woven.astype(jnp.bfloat16).reshape(2 * wide_y, cup, 2 * wide_z)


def local_step(plane, total, vols, starts, weights, bias, up):
    cin = sum(vol.shape[2] for vol in vols)
    wide_y, wide_z = vols[0].shape[1], vols[0].shape[3]
    cup, cout = up.shape[1], up.shape[2]
    scalars = jnp.stack([plane, *starts]).astype(jnp.int32)
    vmem = pl.BlockSpec(memory_space=pltpu.VMEM)
    return pl.pallas_call(
        functools.partial(body, len(vols), total),
        out_shape=jax.ShapeDtypeStruct((2, 2 * wide_y, cup, 2 * wide_z), jnp.bfloat16),
        in_specs=[pl.BlockSpec(memory_space=pltpu.SMEM)] + [vmem] * (2 * len(vols) + 2),
        out_specs=vmem,
        scratch_shapes=[
            pltpu.VMEM((4, wide_y + 2, cin, wide_z), jnp.bfloat16),
            pltpu.VMEM((9, 3 * cout, cin), jnp.bfloat16),
            pltpu.VMEM((2 * cout, wide_y * wide_z), jnp.bfloat16),
        ],
        compiler_params=pltpu.CompilerParams(vmem_limit_bytes=40 * 2**20),
        cost_estimate=pl.CostEstimate(flops=4 * 10**9, bytes_accessed=6 * 10**6, transcendentals=0),
    )(scalars, *vols, *weights, bias[None, :], up)


def per_device(volume, conv_weight, conv_bias, tconv_weight):
    total, size = volume.shape[0], lax.axis_size("gx")
    assert total == size and size % TILE == 0
    me = lax.axis_index("gx")
    tiles = size // TILE
    tile, side, core = me // TILE, me // 2 % 2, me % 2
    vol = jnp.transpose(volume, (0, 2, 1, 3))
    weight = jnp.transpose(conv_weight, (1, 0, 2))

    def cut(block, start, first, count):
        return lax.dynamic_slice_in_dim(block, window(first, count, total) - start, count, 0)

    def first_of(tile_at):
        return TILE * tile_at - 1

    def swap(block, bit):
        return lax.ppermute(block, "gx", [(i, i ^ bit) for i in range(size)])

    wide = min(7, total)
    start = window(first_of(tile), wide, total)
    vols = [cut(vol, 0, first_of(tile), wide)]
    weights = [weight]
    for step in range(1, tiles):
        there = (tile + step) % tiles
        route = [(i, (i + TILE * step) % size) for i in range(size)]
        vols.append(lax.ppermute(cut(vol, 0, first_of(there), wide), "gx", route))
        weights.append(lax.ppermute(weight, "gx", route))
    theirs = TILE * tile + 2 * (1 - side) - 1
    own = TILE * tile + 2 * side - 1
    start5 = window(own, 5, total)
    far_vols = [swap(cut(v, start, theirs, 5), 2) for v in vols]
    far_weights = [swap(w, 2) for w in weights]
    near = [cut(v, start, own, 5) for v in vols]
    vols, weights = near + far_vols, weights + far_weights
    core_vols = [swap(cut(v, start5, (me ^ 1) - 1, 4), 1) for v in vols]
    core_weights = [swap(w, 1) for w in weights]
    starts = [start5] * len(vols) + [window(me - 1, 4, total)] * len(core_vols)
    out = local_step(me, total, vols + core_vols, starts, weights + core_weights, conv_bias, tconv_weight)
    return jnp.transpose(out, (0, 2, 1, 3))


def solution(mesh):
    return jax.shard_map(
        per_device,
        mesh=mesh,
        in_specs=(P("groups", "gx", None, None), P("gx", None, None), P(), P()),
        out_specs=P(("groups", "gx"), None, None, None),
        check_vma=False,
    )
```

```python
import functools

import jax
import jax.numpy as jnp
from jax import lax
from jax.experimental import pallas as pl
from jax.experimental.pallas import tpu as pltpu
from jax.sharding import PartitionSpec as P

TILE = 4
VMEM = pl.BlockSpec(memory_space=pltpu.VMEM)
SMEM = pl.BlockSpec(memory_space=pltpu.SMEM)


def window(first, count, total):
    return jnp.clip(first, 0, total - count)


def conv_body(order, span, total, scalars, *refs):
    steps = len(order)
    vols, fars, weights = refs[:steps], refs[steps : steps + 2], refs[steps + 2 : -4]
    keep_ref, send_ref, cells, taps = refs[-4:]
    core, group, first = scalars[0], scalars[1], scalars[2]
    slots, wide_y, wide_z = cells.shape[0], cells.shape[1] - 2, cells.shape[3]
    chans = vols[0].shape[2]
    cout, cin = taps.shape[0] // 3, cells.shape[2]
    blank = jnp.zeros((slots, cin, wide_z), cells.dtype)
    cells[:, 0] = blank
    cells[:, wide_y + 1] = blank
    half = steps // 2
    for slot in range(slots):
        at = first + slot
        inside = jnp.logical_and(at >= 0, at < total)
        for place, step in enumerate(order):
            near = vols[place]
            far = fars[step // half].at[step % half]
            for base, ref, start in ((0, near, scalars[3 + place]), (steps, far, scalars[3 + steps])):
                held = ref[jnp.clip(at - start, 0, ref.shape[0] - 1)]
                row = (base + place) * chans
                cells[slot, 1 : wide_y + 1, row : row + chans] = jnp.where(inside, held, jnp.zeros_like(held))
    for tap in range(27):
        part = tap // span
        start = min(part * span, 27 - span)
        pieces = []
        for column in range(2):
            for place in range(steps):
                pieces.append(weights[column][group ^ part, place, tap - start])
        block = jnp.concatenate(pieces, axis=0)
        at = tap // 3 * cin
        taps[tap % 3 * cout : (tap % 3 + 1) * cout, at : at + cin] = block.T
    lane = lax.broadcasted_iota(jnp.int32, (cout, wide_z), 1)
    for which in range(3):
        if which == 0:
            base, targets = 1, ((keep_ref, 1 - core), (send_ref, core))
        elif which == 1:
            base, targets = 2 * (1 - core), ((send_ref, 1 - core),)
        else:
            base, targets = 2 * core, ((keep_ref, core),)
        for pair in range(wide_y // 2):
            blocks = []
            for tap_x in range(3):
                for tap_y in range(3):
                    at = 2 * pair + tap_y
                    blocks.append(jnp.concatenate([cells[base + tap_x, at], cells[base + tap_x, at + 1]], axis=1))
            acc = jnp.dot(taps[...], jnp.concatenate(blocks, axis=0), preferred_element_type=jnp.float32)
            for side in range(2):
                cut = acc[:, side * wide_z : (side + 1) * wide_z]
                low = jnp.where(lane == 0, 0.0, pltpu.roll(cut[:cout], 1, 1))
                high = jnp.where(lane == wide_z - 1, 0.0, pltpu.roll(cut[2 * cout :], wide_z - 1, 1))
                summed = cut[cout : 2 * cout] + low + high
                for ref, index in targets:
                    ref[index, 2 * pair + side] = summed


def up_body(total, scalars, keep_ref, came_ref, bias_ref, up_ref, out_ref):
    plane = scalars[0]
    wide_y, cout, wide_z = keep_ref.shape[1:]
    cup = up_ref.shape[1]
    eye = lax.broadcasted_iota(jnp.int32, (cout, cout), 0) == lax.broadcasted_iota(jnp.int32, (cout, cout), 1)
    bias = jnp.sum(jnp.where(eye, bias_ref[...], 0.0), axis=1, keepdims=True)
    hidden = []
    for ahead in range(2):
        rows = []
        for y in range(wide_y):
            value = jnp.maximum(keep_ref[ahead, y] + came_ref[ahead, y] + bias, 0.0)
            if ahead:
                value = jnp.where(plane + 1 < total, value, 0.0)
            rows.append(value.astype(jnp.bfloat16))
        hidden.append(jnp.concatenate(rows, axis=1))
    shape = (2 * wide_z, 2 * wide_z)
    source, target = (lax.broadcasted_iota(jnp.int32, shape, axis) for axis in range(2))
    weave = (target == 2 * (source % wide_z) + source // wide_z).astype(jnp.bfloat16)
    edge = lax.broadcasted_iota(jnp.int32, (cup, wide_z), 1) == wide_z - 1

    def later(value):
        return jnp.where(edge, 0.0, pltpu.roll(value, wide_z - 1, 1))

    for odd in range(2):
        if odd:
            left = jnp.concatenate([up_ref[18:27].reshape(9 * cup, cout), up_ref[0:9].reshape(9 * cup, cout)], axis=1)
            right = jnp.concatenate(hidden, axis=0)
        else:
            left = up_ref[9:18].reshape(9 * cup, cout)
            right = hidden[0]
        product = jnp.dot(left, right, preferred_element_type=jnp.float32)

        def term(tap_y, tap_z, y):
            at = (3 * tap_y + tap_z) * cup
            return product[at : at + cup, y * wide_z : (y + 1) * wide_z]

        lines = []
        for y in range(wide_y):
            for par_y in range(2):
                choices = [(1, y)] if par_y == 0 else [(2, y)] + ([(0, y + 1)] if y + 1 < wide_y else [])
                even = sum(term(tap_y, 1, at) for tap_y, at in choices)
                plain = sum(term(tap_y, 2, at) for tap_y, at in choices)
                moved = sum(term(tap_y, 0, at) for tap_y, at in choices)
                lines.append(jnp.concatenate([even, plain + later(moved)], axis=1).astype(jnp.bfloat16))
        woven = jnp.dot(jnp.concatenate(lines, axis=0), weave, preferred_element_type=jnp.float32)
        out_ref[odd] = woven.astype(jnp.bfloat16).reshape(2 * wide_y, cup, 2 * wide_z)


def partial_sums(order, span, total, scalars, vols, fars, weights, cout):
    _, wide_y, chans, wide_z = vols[0].shape
    cin = 2 * len(order) * chans
    shape = jax.ShapeDtypeStruct((2, wide_y, cout, wide_z), jnp.float32)
    return pl.pallas_call(
        functools.partial(conv_body, order, span, total),
        out_shape=(shape, shape),
        in_specs=[SMEM] + [VMEM] * (len(vols) + len(fars) + len(weights)),
        out_specs=(VMEM, VMEM),
        scratch_shapes=[
            pltpu.VMEM((5, wide_y + 2, cin, wide_z), jnp.bfloat16),
            pltpu.VMEM((3 * cout, 9 * cin), jnp.bfloat16),
        ],
        compiler_params=pltpu.CompilerParams(vmem_limit_bytes=24 * 2**20),
        cost_estimate=pl.CostEstimate(flops=2 * 10**9, bytes_accessed=4 * 10**6, transcendentals=0),
    )(scalars, *vols, *fars, *weights)


def upsample(total, plane, keep, came, bias, up):
    _, wide_y, _, wide_z = keep.shape
    return pl.pallas_call(
        functools.partial(up_body, total),
        out_shape=jax.ShapeDtypeStruct((2, 2 * wide_y, up.shape[1], 2 * wide_z), jnp.bfloat16),
        in_specs=[SMEM] + [VMEM] * 4,
        out_specs=VMEM,
        compiler_params=pltpu.CompilerParams(vmem_limit_bytes=24 * 2**20),
        cost_estimate=pl.CostEstimate(flops=10**9, bytes_accessed=3 * 10**6, transcendentals=0),
    )(jnp.reshape(plane, (1,)).astype(jnp.int32), keep, came, bias[None, :], up)


def per_device(volume, conv_weight, conv_bias, tconv_weight):
    total, size, groups = volume.shape[0], lax.axis_size("gx"), lax.axis_size("groups")
    tiles = size // TILE
    assert total == size and size % TILE == 0 and tiles & (tiles - 1) == 0 and groups & (groups - 1) == 0
    me, group = lax.axis_index("gx"), lax.axis_index("groups")
    tile, side, core = me // TILE, me // 2 % 2, me % 2
    vol = jnp.transpose(volume, (0, 2, 1, 3))
    weight = jnp.transpose(conv_weight, (1, 0, 2))
    cout = weight.shape[2]

    def cut(block, start, first, count):
        return lax.dynamic_slice_in_dim(block, window(first, count, total) - start, count, 0)

    def swap(block, mask):
        return lax.ppermute(block, "gx", [(i, i ^ mask) for i in range(size)])

    def cross(block, mask):
        return lax.ppermute(block, "groups", [(i, i ^ mask) for i in range(groups)])

    span = -(-27 // groups)
    held = lax.dynamic_slice_in_dim(weight, jnp.minimum(group * span, 27 - span), span, 0)[None]
    order, bit = [0], tiles // 2
    wide = min(7, total)
    came = {}

    def fetch(step):
        there = TILE * (tile ^ step) - 1
        came[step] = swap(cut(vol, 0, there, wide), TILE * step)

    while bit:
        held = jnp.concatenate([held, swap(held, TILE * bit)], axis=0)
        order = order + [place ^ bit for place in order]
        bit //= 2
    for step in reversed(range(1, tiles)):
        fetch(step)
    far = swap(held, 2)
    columns = [[held], [far]]
    for mask in range(1, groups):
        for column in columns:
            column.append(cross(column[0], mask))
    weights = [jnp.stack(column, axis=0) for column in columns]
    start = window(TILE * tile - 1, wide, total)
    theirs = TILE * tile + 2 * (1 - side) - 1
    own = TILE * tile + 2 * side - 1
    half = tiles // 2
    fars = []
    for steps in (range(half), range(half, tiles)):
        pieces = [cut(came[step], start, theirs, 5) if step else cut(vol, 0, theirs, 5) for step in steps]
        fars.append(swap(jnp.stack(pieces, axis=0), 2))
    vols = [came[step] if step else vol for step in order]
    starts = [start if step else jnp.zeros_like(start) for step in order]
    scalars = jnp.stack([core, group, own, *starts, window(own, 5, total)]).astype(jnp.int32)
    keep, send = partial_sums(tuple(order), span, total, scalars, vols, fars, weights, cout)
    out = upsample(total, me, keep, swap(send, 1), conv_bias, tconv_weight)
    return jnp.transpose(out, (0, 2, 1, 3))


def solution(mesh):
    return jax.shard_map(
        per_device,
        mesh=mesh,
        in_specs=(P("groups", "gx", None, None), P("gx", None, None), P(), P()),
        out_specs=P(("groups", "gx"), None, None, None),
        check_vma=False,
    )
```

```python
import functools

import jax
import jax.numpy as jnp
from jax import lax
from jax.experimental import pallas as pl
from jax.experimental.pallas import tpu as pltpu
from jax.sharding import PartitionSpec as P

TILE = 4
VMEM = pl.BlockSpec(memory_space=pltpu.VMEM)
SMEM = pl.BlockSpec(memory_space=pltpu.SMEM)
PARAMS = pltpu.CompilerParams(vmem_limit_bytes=16 * 2**20)


def window(first, count, total):
    return jnp.clip(first, 0, total - count)


def after(value, *earlier):
    return lax.optimization_barrier((value, *earlier))[0]


def cut_body(counts, scalars, vol_ref, *outs):
    for at, (out_ref, count) in enumerate(zip(outs, counts)):
        out_ref[...] = vol_ref[pl.ds(scalars[at], count)]


def cuts(vol, starts, counts):
    return pl.pallas_call(
        functools.partial(cut_body, counts),
        out_shape=[jax.ShapeDtypeStruct((count, *vol.shape[1:]), vol.dtype) for count in counts],
        in_specs=[SMEM, VMEM],
        out_specs=[VMEM] * len(counts),
        compiler_params=PARAMS,
    )(jnp.stack(starts).astype(jnp.int32), vol)


def taps_body(near_order, far_order, span, scalars, *refs):
    weights, out_ref = refs[:-1], refs[-1]
    group = scalars[0]
    cout = out_ref.shape[0] // 3
    for tap_z in range(3):
        pieces = []
        for tap in range(tap_z, 27, 3):
            part = tap // span
            start = min(part * span, 27 - span)
            for weight, order in zip(weights, (near_order, far_order)):
                pieces += [weight[group ^ part, place, tap - start] for place in order]
        out_ref[tap_z * cout : (tap_z + 1) * cout] = jnp.concatenate(pieces, axis=0).T


def taps_of(near_order, far_order, span, group, weights):
    cout, chans = weights[0].shape[-1], weights[0].shape[-2]
    columns = 9 * chans * (len(near_order) + len(far_order))
    return pl.pallas_call(
        functools.partial(taps_body, near_order, far_order, span),
        out_shape=jax.ShapeDtypeStruct((3 * cout, columns), jnp.bfloat16),
        in_specs=[SMEM] + [VMEM] * len(weights),
        out_specs=VMEM,
        compiler_params=PARAMS,
        cost_estimate=pl.CostEstimate(flops=0, bytes_accessed=3 * 10**6, transcendentals=0),
    )(jnp.reshape(group, (1,)).astype(jnp.int32), *weights)


def conv_rows(total, steps, scalars, refs, taps, plane, store):
    near, far = refs[:steps], [ref.at[at] for ref in refs[steps:] for at in range(ref.shape[0])]
    parts = [*near, *far]
    _, wide_y, chans, wide_z = near[0].shape
    cout = taps.shape[0] // 3
    lane = lax.broadcasted_iota(jnp.int32, (cout, wide_z), 1)
    zeros = jnp.zeros((len(parts) * chans, wide_z), taps.dtype)

    def row(at, y):
        if not 0 <= y < wide_y:
            return zeros
        held = [ref[jnp.clip(at - scalars[2 + place], 0, ref.shape[0] - 1), y] for place, ref in enumerate(parts)]
        return jnp.where(jnp.logical_and(at >= 0, at < total), jnp.concatenate(held, axis=0), zeros)

    for pair in range(0, wide_y, 2):
        blocks = []
        for tap_x in range(3):
            for tap_y in range(3):
                y = pair + tap_y - 1
                blocks.append(jnp.concatenate([row(plane + tap_x - 1, y), row(plane + tap_x - 1, y + 1)], axis=1))
        acc = jnp.dot(taps[...], jnp.concatenate(blocks, axis=0), preferred_element_type=jnp.float32)
        for side in range(2):
            part = acc[:, side * wide_z : (side + 1) * wide_z]
            low = jnp.where(lane == 0, 0.0, pltpu.roll(part[:cout], 1, 1))
            high = jnp.where(lane == wide_z - 1, 0.0, pltpu.roll(part[2 * cout :], wide_z - 1, 1))
            store(pair + side, part[cout : 2 * cout] + low + high)


def send_body(total, steps, scalars, *refs):
    *parts, taps, out_ref = refs
    core, first = scalars[0], scalars[1]
    for at, plane in enumerate((first + 1, first + 2 * (1 - core))):

        def store(y, value, at=at):
            out_ref[at, y] = value

        conv_rows(total, steps, scalars, parts, taps, plane, store)


def keep_body(total, steps, scalars, *refs):
    *parts, taps, shared_ref, bias_ref, out_ref = refs
    core, first = scalars[0], scalars[1]
    bias = bias_ref[...]
    plane = first + 2 * core
    inside = plane < total

    def store(y, value):
        out_ref[core, y] = jnp.where(inside, value + bias, -jnp.inf)
        out_ref[1 - core, y] = shared_ref[0, y] + bias

    conv_rows(total, steps, scalars, parts, taps, plane, store)


def conv_call(body, total, steps, scalars, parts, taps, *more):
    _, wide_y, _, wide_z = parts[0].shape
    cout = taps.shape[0] // 3
    return pl.pallas_call(
        functools.partial(body, total, steps),
        out_shape=jax.ShapeDtypeStruct((2, wide_y, cout, wide_z), jnp.float32),
        in_specs=[SMEM] + [VMEM] * (len(parts) + 1 + len(more)),
        out_specs=VMEM,
        compiler_params=PARAMS,
        cost_estimate=pl.CostEstimate(flops=10**9, bytes_accessed=4 * 10**6, transcendentals=0),
    )(scalars, *parts, taps, *more)


def up_body(scalars, keep_ref, came_ref, up_ref, out_ref):
    core = scalars[0]
    _, wide_y, cout, wide_z = keep_ref.shape
    cup = up_ref.shape[1]
    hidden = []
    for ahead in range(2):
        at = jnp.where(core == ahead, 1, 0)
        rows = [jnp.maximum(keep_ref[ahead, y] + came_ref[at, y], 0.0).astype(jnp.bfloat16) for y in range(wide_y)]
        hidden.append(jnp.concatenate(rows, axis=1))
    shape = (2 * wide_z, 2 * wide_z)
    source, target = (lax.broadcasted_iota(jnp.int32, shape, axis) for axis in range(2))
    weave = (target == 2 * (source % wide_z) + source // wide_z).astype(jnp.bfloat16)
    edge = lax.broadcasted_iota(jnp.int32, (cup, wide_z), 1) == wide_z - 1

    def later(value):
        return jnp.where(edge, 0.0, pltpu.roll(value, wide_z - 1, 1))

    for odd in range(2):
        if odd:
            left = jnp.concatenate([up_ref[18:27].reshape(9 * cup, cout), up_ref[0:9].reshape(9 * cup, cout)], axis=1)
            right = jnp.concatenate(hidden, axis=0)
        else:
            left = up_ref[9:18].reshape(9 * cup, cout)
            right = hidden[0]
        product = jnp.dot(left, right, preferred_element_type=jnp.float32)

        def term(tap_y, tap_z, y):
            at = (3 * tap_y + tap_z) * cup
            return product[at : at + cup, y * wide_z : (y + 1) * wide_z]

        lines = []
        for y in range(wide_y):
            for par_y in range(2):
                choices = [(1, y)] if par_y == 0 else [(2, y)] + ([(0, y + 1)] if y + 1 < wide_y else [])
                even = sum(term(tap_y, 1, at) for tap_y, at in choices)
                plain = sum(term(tap_y, 2, at) for tap_y, at in choices)
                moved = sum(term(tap_y, 0, at) for tap_y, at in choices)
                lines.append(jnp.concatenate([even, plain + later(moved)], axis=1).astype(jnp.bfloat16))
        woven = jnp.dot(jnp.concatenate(lines, axis=0), weave, preferred_element_type=jnp.float32)
        out_ref[odd] = woven.astype(jnp.bfloat16).reshape(2 * wide_y, cup, 2 * wide_z)


def upsample(scalars, keep, came, up):
    _, wide_y, _, wide_z = keep.shape
    return pl.pallas_call(
        up_body,
        out_shape=jax.ShapeDtypeStruct((2, 2 * wide_y, up.shape[1], 2 * wide_z), jnp.bfloat16),
        in_specs=[SMEM] + [VMEM] * 3,
        out_specs=VMEM,
        compiler_params=PARAMS,
        cost_estimate=pl.CostEstimate(flops=10**9, bytes_accessed=3 * 10**6, transcendentals=0),
    )(scalars, keep, came, up)


def per_device(volume, conv_weight, conv_bias, tconv_weight):
    total, size, groups = volume.shape[0], lax.axis_size("gx"), lax.axis_size("groups")
    tiles = size // TILE
    assert total == size and size % TILE == 0 and tiles & (tiles - 1) == 0 and groups & (groups - 1) == 0
    me, group = lax.axis_index("gx"), lax.axis_index("groups")
    tile, side, core = me // TILE, me // 2 % 2, me % 2
    vol = jnp.transpose(volume, (0, 2, 1, 3))
    weight = jnp.transpose(conv_weight, (1, 0, 2))

    def swap(block, mask):
        return lax.ppermute(block, "gx", [(i, i ^ mask) for i in range(size)])

    def cross(block, mask):
        return lax.ppermute(block, "groups", [(i, i ^ mask) for i in range(groups)])

    wide = min(7, total)
    start = window(TILE * tile - 1, wide, total)
    theirs = window(TILE * tile + 2 * (1 - side) - 1, 5, total)
    own = TILE * tile + 2 * side
    steps = range(tiles)
    firsts = [window(TILE * (tile ^ step) - 1, wide, total) for step in steps[1:]]
    far_own, *pieces = cuts(vol, [theirs, *firsts], [5] + [wide] * (tiles - 1))
    span = -(-27 // groups)
    held = lax.dynamic_slice_in_dim(weight, jnp.minimum(group * span, 27 - span), span, 0)
    held, bias, *pieces = lax.optimization_barrier(
        (held, jnp.broadcast_to(conv_bias[:, None], (weight.shape[2], vol.shape[3])), *pieces)
    )
    held = jnp.stack([held] + [swap(held, TILE * step) for step in steps[1:]], axis=0)
    near = [vol]
    for step, piece in zip(steps[1:], pieces):
        near.append(swap(after(piece, held) if step % 4 == 2 else piece, TILE * step))
    far_held = swap(held, 2)
    columns = [jnp.stack([part] + [cross(part, mask) for mask in range(1, groups)], axis=0) for part in (held, far_held)]
    far_order = [[0, 1]] + [[step] for step in steps[2:]]
    far = []
    for chosen in far_order:
        cut = [lax.dynamic_slice_in_dim(near[step], theirs - start, 5, 0) if step else far_own for step in chosen]
        far.append(swap(jnp.stack(cut, axis=0), 2))
    taps = taps_of(tuple(steps), tuple(step for chosen in far_order for step in chosen), span, group, columns)
    starts = [jnp.zeros_like(start)] + [start] * (tiles - 1) + [window(own - 1, 5, total)] * tiles
    scalars = jnp.stack([core, own, *starts]).astype(jnp.int32)
    parts = near + far
    shared = conv_call(send_body, total, tiles, scalars, parts, taps)
    came = swap(shared, 1)
    keep = conv_call(keep_body, total, tiles, scalars, parts, taps, shared, bias)
    out = upsample(scalars[:1], keep, came, tconv_weight)
    return jnp.transpose(out, (0, 2, 1, 3))


def solution(mesh):
    return jax.shard_map(
        per_device,
        mesh=mesh,
        in_specs=(P("groups", "gx", None, None), P("gx", None, None), P(), P()),
        out_specs=P(("groups", "gx"), None, None, None),
        check_vma=False,
    )
```

```python
import functools

import jax
import jax.numpy as jnp
from jax import lax
from jax.experimental import pallas as pl
from jax.experimental.pallas import tpu as pltpu
from jax.sharding import PartitionSpec as P

TILE = 4
VMEM = pl.BlockSpec(memory_space=pltpu.VMEM)
PARAMS = pltpu.CompilerParams(vmem_limit_bytes=16 * 2**20)


def window(first, count, total):
    return jnp.clip(first, 0, total - count)


def chip_first():
    return lax.axis_index("gx") // 2 * 2


def tile_start(total, mask=0):
    return window(TILE * (lax.axis_index("gx") // TILE ^ mask) - 1, min(7, total), total)


def chip_start(total, mask=0):
    return window((chip_first() ^ mask) - 1, 5, total)


def after(value, *earlier):
    return lax.optimization_barrier((value, *earlier))[0]


def cut_body(starts, counts, vol_ref, *outs):
    for out_ref, start, count in zip(outs, starts(), counts):
        out_ref[...] = vol_ref[pl.ds(start, count)]


def cuts(vol, starts, counts):
    return pl.pallas_call(
        functools.partial(cut_body, starts, counts),
        out_shape=[jax.ShapeDtypeStruct((count, *vol.shape[1:]), vol.dtype) for count in counts],
        in_specs=[VMEM],
        out_specs=[VMEM] * len(counts),
        compiler_params=PARAMS,
    )(vol)


def taps_body(near_order, far_order, span, *refs):
    weights, out_ref = refs[:-1], refs[-1]
    group = lax.axis_index("groups")
    cout = out_ref.shape[0] // 3
    for tap_z in range(3):
        pieces = []
        for tap in range(tap_z, 27, 3):
            part = tap // span
            start = min(part * span, 27 - span)
            for weight, order in zip(weights, (near_order, far_order)):
                pieces += [weight[group ^ part, place, tap - start] for place in order]
        out_ref[tap_z * cout : (tap_z + 1) * cout] = jnp.concatenate(pieces, axis=0).T


def taps_of(near_order, far_order, span, weights):
    cout, chans = weights[0].shape[-1], weights[0].shape[-2]
    columns = 9 * chans * (len(near_order) + len(far_order))
    return pl.pallas_call(
        functools.partial(taps_body, near_order, far_order, span),
        out_shape=jax.ShapeDtypeStruct((3 * cout, columns), jnp.bfloat16),
        in_specs=[VMEM] * len(weights),
        out_specs=VMEM,
        compiler_params=PARAMS,
        cost_estimate=pl.CostEstimate(flops=0, bytes_accessed=3 * 10**6, transcendentals=0),
    )(*weights)


def conv_planes(total, kinds, refs, taps, first, stores):
    steps = len(kinds)
    parts = [*refs[:steps], *(ref.at[at] for ref in refs[steps:] for at in range(ref.shape[0]))]
    _, wide_y, chans, wide_z = parts[0].shape
    cout = taps.shape[0] // 3
    lane = lax.broadcasted_iota(jnp.int32, (cout, wide_z), 1)
    zeros = jnp.zeros((len(parts) * chans, wide_z), taps.dtype)
    by_kind = {"all": 0, "tile": tile_start(total), "chip": chip_start(total)}
    starts = [by_kind[kind] for kind in kinds] + [by_kind["chip"]] * steps
    rows = {(slot, y): zeros for slot in range(len(stores) + 2) for y in (-1, wide_y)}
    for slot in range(len(stores) + 2):
        at = first - 1 + slot
        inside = jnp.logical_and(at >= 0, at < total)
        index = [jnp.clip(at - starts[place], 0, ref.shape[0] - 1) for place, ref in enumerate(parts)]
        for y in range(wide_y):
            held = jnp.concatenate([ref[index[place], y] for place, ref in enumerate(parts)], axis=0)
            rows[slot, y] = jnp.where(inside, held, zeros)
    for plane, store in enumerate(stores):
        for pair in range(0, wide_y, 2):
            blocks = []
            for tap_x in range(3):
                for y in range(pair - 1, pair + 2):
                    blocks.append(jnp.concatenate([rows[plane + tap_x, y], rows[plane + tap_x, y + 1]], axis=1))
            acc = jnp.dot(taps[...], jnp.concatenate(blocks, axis=0), preferred_element_type=jnp.float32)
            for side in range(2):
                part = acc[:, side * wide_z : (side + 1) * wide_z]
                low = jnp.where(lane == 0, 0.0, pltpu.roll(part[:cout], 1, 1))
                high = jnp.where(lane == wide_z - 1, 0.0, pltpu.roll(part[2 * cout :], wide_z - 1, 1))
                store(pair + side, part[cout : 2 * cout] + low + high)


def send_body(total, kinds, *refs):
    *parts, taps, out_ref = refs
    core = lax.axis_index("gx") % 2

    def lower(y, value):
        out_ref[core, y] = value

    def upper(y, value):
        out_ref[1 - core, y] = value

    conv_planes(total, kinds, parts, taps, chip_first() + 1 - core, (lower, upper))


def keep_body(total, kinds, *refs):
    *parts, taps, shared_ref, bias_ref, out_ref = refs
    core = lax.axis_index("gx") % 2
    bias = bias_ref[...]
    plane = chip_first() + 2 * core
    inside = plane < total

    def store(y, value):
        out_ref[core, y] = jnp.where(inside, value + bias, -jnp.inf)
        out_ref[1 - core, y] = shared_ref[0, y] + bias

    conv_planes(total, kinds, parts, taps, plane, (store,))


def conv_call(body, total, kinds, parts, taps, *more):
    _, wide_y, _, wide_z = parts[0].shape
    cout = taps.shape[0] // 3
    return pl.pallas_call(
        functools.partial(body, total, kinds),
        out_shape=jax.ShapeDtypeStruct((2, wide_y, cout, wide_z), jnp.float32),
        in_specs=[VMEM] * (len(parts) + 1 + len(more)),
        out_specs=VMEM,
        compiler_params=PARAMS,
        cost_estimate=pl.CostEstimate(flops=10**9, bytes_accessed=4 * 10**6, transcendentals=0),
    )(*parts, taps, *more)


def up_body(keep_ref, came_ref, up_ref, out_ref):
    core = lax.axis_index("gx") % 2
    _, wide_y, cout, wide_z = keep_ref.shape
    cup = up_ref.shape[1]
    hidden = []
    for ahead in range(2):
        at = jnp.where(core == ahead, 1, 0)
        rows = [jnp.maximum(keep_ref[ahead, y] + came_ref[at, y], 0.0).astype(jnp.bfloat16) for y in range(wide_y)]
        hidden.append(jnp.concatenate(rows, axis=1))
    shape = (2 * wide_z, 2 * wide_z)
    source, target = (lax.broadcasted_iota(jnp.int32, shape, axis) for axis in range(2))
    weave = (target == 2 * (source % wide_z) + source // wide_z).astype(jnp.bfloat16)
    edge = lax.broadcasted_iota(jnp.int32, (cup, wide_z), 1) == wide_z - 1

    def later(value):
        return jnp.where(edge, 0.0, pltpu.roll(value, wide_z - 1, 1))

    for odd in range(2):
        if odd:
            left = jnp.concatenate([up_ref[18:27].reshape(9 * cup, cout), up_ref[0:9].reshape(9 * cup, cout)], axis=1)
            right = jnp.concatenate(hidden, axis=0)
        else:
            left = up_ref[9:18].reshape(9 * cup, cout)
            right = hidden[0]
        product = jnp.dot(left, right, preferred_element_type=jnp.float32)

        def term(tap_y, tap_z, y):
            at = (3 * tap_y + tap_z) * cup
            return product[at : at + cup, y * wide_z : (y + 1) * wide_z]

        lines = []
        for y in range(wide_y):
            for par_y in range(2):
                choices = [(1, y)] if par_y == 0 else [(2, y)] + ([(0, y + 1)] if y + 1 < wide_y else [])
                even = sum(term(tap_y, 1, at) for tap_y, at in choices)
                plain = sum(term(tap_y, 2, at) for tap_y, at in choices)
                moved = sum(term(tap_y, 0, at) for tap_y, at in choices)
                lines.append(jnp.concatenate([even, plain + later(moved)], axis=1).astype(jnp.bfloat16))
        woven = jnp.dot(jnp.concatenate(lines, axis=0), weave, preferred_element_type=jnp.float32)
        out_ref[odd] = woven.astype(jnp.bfloat16).reshape(2 * wide_y, cup, 2 * wide_z)


def upsample(keep, came, up):
    _, wide_y, _, wide_z = keep.shape
    return pl.pallas_call(
        up_body,
        out_shape=jax.ShapeDtypeStruct((2, 2 * wide_y, up.shape[1], 2 * wide_z), jnp.bfloat16),
        in_specs=[VMEM] * 3,
        out_specs=VMEM,
        compiler_params=PARAMS,
        cost_estimate=pl.CostEstimate(flops=10**9, bytes_accessed=3 * 10**6, transcendentals=0),
    )(keep, came, up)


def per_device(volume, conv_weight, conv_bias, tconv_weight):
    total, size, groups = volume.shape[0], lax.axis_size("gx"), lax.axis_size("groups")
    tiles = size // TILE
    assert total == size and size % TILE == 0 and tiles & (tiles - 1) == 0 and groups & (groups - 1) == 0
    group = lax.axis_index("groups")
    vol = jnp.transpose(volume, (0, 2, 1, 3))
    weight = jnp.transpose(conv_weight, (1, 0, 2))

    def swap(block, mask):
        return lax.ppermute(block, "gx", [(i, i ^ mask) for i in range(size)])

    def cross(block, mask):
        return lax.ppermute(block, "groups", [(i, i ^ mask) for i in range(groups)])

    wide = min(7, total)
    steps = range(tiles)

    straight = {step for step in steps if step % 4 == 2}
    counts = [5] + [count for step in steps[1:] for count in ([5, 5] if step in straight else [wide])]

    def starts():
        found = [chip_start(total, 2)]
        for step in steps[1:]:
            mask = TILE * step
            found += [chip_start(total, mask), chip_start(total, mask ^ 2)] if step in straight else [tile_start(total, step)]
        return found

    pieces = cuts(vol, starts, counts)
    span = -(-27 // groups)
    held = lax.dynamic_slice_in_dim(weight, jnp.minimum(group * span, 27 - span), span, 0)
    held, *pieces = lax.optimization_barrier((held, *pieces))
    far_own, *pieces = pieces
    held = jnp.stack([held] + [swap(held, TILE * step) for step in steps[1:]], axis=0)
    near, far, far_order = {0: vol}, [], []
    for step in steps[1:]:
        if step in straight:
            near[step] = swap(after(pieces.pop(0), held), TILE * step)
            far.append(swap(after(pieces.pop(0), held), TILE * step ^ 2)[None])
            far_order.append([step])
        else:
            near[step] = swap(pieces.pop(0), TILE * step)
    far_held = swap(held, 2)
    columns = [jnp.stack([part] + [cross(part, mask) for mask in range(1, groups)], axis=0) for part in (held, far_held)]
    partner = chip_start(total, 2) - tile_start(total)
    for chosen in ([0, *steps[1::4]], [*steps[3::4]]):
        cut = [lax.dynamic_slice_in_dim(near[step], partner, 5, 0) if step else far_own for step in chosen]
        far.append(swap(jnp.stack(cut, axis=0), 2))
        far_order.append(chosen)
    kinds = tuple("all" if step == 0 else "chip" if step in straight else "tile" for step in steps)
    near = [near[step] for step in steps]
    bias = jnp.broadcast_to(conv_bias[:, None], (weight.shape[2], vol.shape[3]))
    far[-2], bias = lax.optimization_barrier((far[-2], bias))
    taps = taps_of(tuple(steps), tuple(step for chosen in far_order for step in chosen), span, columns)
    parts = near + far
    shared = conv_call(send_body, total, kinds, parts, taps)
    came = swap(shared, 1)
    keep = conv_call(keep_body, total, kinds, parts, taps, shared, bias)
    out = upsample(keep, came, tconv_weight)
    return jnp.transpose(out, (0, 2, 1, 3))


def solution(mesh):
    return jax.shard_map(
        per_device,
        mesh=mesh,
        in_specs=(P("groups", "gx", None, None), P("gx", None, None), P(), P()),
        out_specs=P(("groups", "gx"), None, None, None),
        check_vma=False,
    )
```

```python
import functools

import jax
import jax.numpy as jnp
from jax import lax
from jax.experimental import pallas as pl
from jax.experimental.pallas import tpu as pltpu
from jax.sharding import PartitionSpec as P

TILE = 4
VMEM = pl.BlockSpec(memory_space=pltpu.VMEM)
PARTS = 3
PARAMS = pltpu.CompilerParams(vmem_limit_bytes=16 * 2**20)


def window(first, count, total):
    return jnp.clip(first, 0, total - count)


def chip_first():
    return lax.axis_index("gx") // 2 * 2


def tile_start(total, mask=0):
    return window(TILE * (lax.axis_index("gx") // TILE ^ mask) - 1, min(7, total), total)


def chip_start(total, mask=0):
    return window((chip_first() ^ mask) - 1, 5, total)


def after(value, *earlier):
    return lax.optimization_barrier((value, *earlier))[0]


def cut_body(starts, counts, vol_ref, *outs):
    for out_ref, start, count in zip(outs, starts(), counts):
        out_ref[...] = vol_ref[pl.ds(start, count)]


def cuts(vol, starts, counts):
    return pl.pallas_call(
        functools.partial(cut_body, starts, counts),
        out_shape=[jax.ShapeDtypeStruct((count, *vol.shape[1:]), vol.dtype) for count in counts],
        in_specs=[VMEM],
        out_specs=[VMEM] * len(counts),
        compiler_params=PARAMS,
    )(vol)


def taps_body(near_order, far_order, span, *refs):
    weights, out_ref = refs[:-1], refs[-1]
    group = lax.axis_index("groups")
    cout = out_ref.shape[0] // 3
    for tap_z in range(3):
        pieces = []
        for tap in range(tap_z, 27, 3):
            part = tap // span
            start = min(part * span, 27 - span)
            for weight, order in zip(weights, (near_order, far_order)):
                pieces += [weight[group ^ part, place, tap - start] for place in order]
        out_ref[tap_z * cout : (tap_z + 1) * cout] = jnp.concatenate(pieces, axis=0).T


def taps_of(near_order, far_order, span, weights):
    cout, chans = weights[0].shape[-1], weights[0].shape[-2]
    columns = 9 * chans * (len(near_order) + len(far_order))
    return pl.pallas_call(
        functools.partial(taps_body, near_order, far_order, span),
        out_shape=jax.ShapeDtypeStruct((3 * cout, columns), jnp.bfloat16),
        in_specs=[VMEM] * len(weights),
        out_specs=VMEM,
        compiler_params=PARAMS,
        cost_estimate=pl.CostEstimate(flops=0, bytes_accessed=3 * 10**6, transcendentals=0),
    )(*weights)


def conv_planes(total, kinds, refs, taps, first, stores):
    steps = len(kinds)
    parts = [*refs[:steps], *(ref.at[at] for ref in refs[steps:] for at in range(ref.shape[0]))]
    _, wide_y, chans, wide_z = parts[0].shape
    cout = taps.shape[0] // 3
    lane = lax.broadcasted_iota(jnp.int32, (cout, wide_z), 1)
    zeros = jnp.zeros((len(parts) * chans, wide_z), taps.dtype)
    by_kind = {"tile": tile_start(total), "chip": chip_start(total)}
    starts = [by_kind[kind] for kind in kinds] + [by_kind["chip"]] * steps
    rows = {(slot, y): zeros for slot in range(len(stores) + 2) for y in (-1, wide_y)}
    for slot in range(len(stores) + 2):
        at = first - 1 + slot
        inside = jnp.logical_and(at >= 0, at < total)
        index = [jnp.clip(at - starts[place], 0, ref.shape[0] - 1) for place, ref in enumerate(parts)]
        for y in range(wide_y):
            held = jnp.concatenate([ref[index[place], y] for place, ref in enumerate(parts)], axis=0)
            rows[slot, y] = jnp.where(inside, held, zeros)
    for plane, store in enumerate(stores):
        for pair in range(0, wide_y, 2):
            blocks = []
            for tap_x in range(3):
                for y in range(pair - 1, pair + 2):
                    blocks.append(jnp.concatenate([rows[plane + tap_x, y], rows[plane + tap_x, y + 1]], axis=1))
            acc = jnp.dot(taps[...], jnp.concatenate(blocks, axis=0), preferred_element_type=jnp.float32)
            for side in range(2):
                part = acc[:, side * wide_z : (side + 1) * wide_z]
                low = jnp.where(lane == 0, 0.0, pltpu.roll(part[:cout], 1, 1))
                high = jnp.where(lane == wide_z - 1, 0.0, pltpu.roll(part[2 * cout :], wide_z - 1, 1))
                store(pair + side, part[cout : 2 * cout] + low + high)


def send_body(total, kinds, *refs):
    *parts, taps, out_ref = refs
    core = lax.axis_index("gx") % 2

    def lower(y, value):
        out_ref[core, y] = value

    def upper(y, value):
        out_ref[1 - core, y] = value

    conv_planes(total, kinds, parts, taps, chip_first() + 1 - core, (lower, upper))


def keep_body(total, kinds, *refs):
    *parts, taps, shared_ref, bias_ref, out_ref = refs
    core = lax.axis_index("gx") % 2
    bias = bias_ref[...]
    plane = chip_first() + 2 * core
    inside = plane < total

    def store(y, value):
        out_ref[core, y] = jnp.where(inside, value + bias, -jnp.inf)
        out_ref[1 - core, y] = shared_ref[0, y] + bias

    conv_planes(total, kinds, parts, taps, plane, (store,))


def conv_call(body, total, kinds, parts, taps, *more):
    _, wide_y, _, wide_z = parts[0].shape
    cout = taps.shape[0] // 3
    return pl.pallas_call(
        functools.partial(body, total, kinds),
        out_shape=jax.ShapeDtypeStruct((2, wide_y, cout, wide_z), jnp.float32),
        in_specs=[VMEM] * (len(parts) + 1 + len(more)),
        out_specs=VMEM,
        compiler_params=PARAMS,
        cost_estimate=pl.CostEstimate(flops=10**9, bytes_accessed=4 * 10**6, transcendentals=0),
    )(*parts, taps, *more)


def up_body(keep_ref, came_ref, up_ref, out_ref, made, sems):
    core = lax.axis_index("gx") % 2
    _, wide_y, cout, wide_z = keep_ref.shape
    cup = up_ref.shape[1]
    hidden = []
    for ahead in range(2):
        at = jnp.where(core == ahead, 1, 0)
        rows = [jnp.maximum(keep_ref[ahead, y] + came_ref[at, y], 0.0).astype(jnp.bfloat16) for y in range(wide_y)]
        hidden.append(jnp.concatenate(rows, axis=1))
    shape = (2 * wide_z, 2 * wide_z)
    source, target = (lax.broadcasted_iota(jnp.int32, shape, axis) for axis in range(2))
    weave = (target == 2 * (source % wide_z) + source // wide_z).astype(jnp.bfloat16)
    edge = lax.broadcasted_iota(jnp.int32, (cup, wide_z), 1) == wide_z - 1

    def later(value):
        return jnp.where(edge, 0.0, pltpu.roll(value, wide_z - 1, 1))

    rest = [jnp.concatenate([value[:, wide_z:], jnp.zeros((cout, wide_z), value.dtype)], axis=1) for value in hidden]

    def taps(*firsts):
        return jnp.concatenate([up_ref[first : first + 3].reshape(3 * cup, cout) for first in firsts], axis=1)

    sides = (
        (taps(12), hidden[:1], taps(15, 9), [hidden[0], rest[0]]),
        (taps(21, 3), hidden, taps(24, 18, 6, 0), [hidden[0], rest[0], hidden[1], rest[1]]),
    )
    copies = []
    for odd, (left, right, left_odd, right_odd) in enumerate(sides):
        products = (
            jnp.dot(left, jnp.concatenate(right, axis=0), preferred_element_type=jnp.float32),
            jnp.dot(left_odd, jnp.concatenate(right_odd, axis=0), preferred_element_type=jnp.float32),
        )
        lines = []
        for y in range(wide_y):
            for product in products:
                moved, even, plain = (
                    product[tap * cup : (tap + 1) * cup, y * wide_z : (y + 1) * wide_z] for tap in range(3)
                )
                lines.append(jnp.concatenate([even, plain + later(moved)], axis=1).astype(jnp.bfloat16))
        share = len(lines) // PARTS
        for part in range(PARTS):
            rows = slice(part * share, (part + 1) * share)
            woven = jnp.dot(jnp.concatenate(lines[rows], axis=0), weave, preferred_element_type=jnp.float32)
            made[odd, rows] = woven.astype(jnp.bfloat16).reshape(share, cup, 2 * wide_z)
            copies.append(pltpu.make_async_copy(made.at[odd, rows], out_ref.at[odd, rows], sems.at[len(copies)]))
            copies[-1].start()
    for copy in copies:
        copy.wait()


def upsample(keep, came, up):
    _, wide_y, _, wide_z = keep.shape
    shape = (2, 2 * wide_y, up.shape[1], 2 * wide_z)
    return pl.pallas_call(
        up_body,
        out_shape=jax.ShapeDtypeStruct(shape, jnp.bfloat16),
        in_specs=[VMEM] * 3,
        out_specs=pl.BlockSpec(memory_space=pl.ANY),
        scratch_shapes=[pltpu.VMEM(shape, jnp.bfloat16), pltpu.SemaphoreType.DMA((2 * PARTS,))],
        compiler_params=PARAMS,
        cost_estimate=pl.CostEstimate(flops=10**9, bytes_accessed=3 * 10**6, transcendentals=0),
    )(keep, came, up)


def per_device(volume, conv_weight, conv_bias, tconv_weight):
    total, size, groups = volume.shape[0], lax.axis_size("gx"), lax.axis_size("groups")
    tiles = size // TILE
    assert total == size and size % TILE == 0 and tiles & (tiles - 1) == 0 and groups & (groups - 1) == 0
    group = lax.axis_index("groups")
    vol = jnp.transpose(volume, (0, 2, 1, 3))
    weight = jnp.transpose(conv_weight, (1, 0, 2))

    def swap(block, mask):
        return lax.ppermute(block, "gx", [(i, i ^ mask) for i in range(size)])

    def cross(block, mask):
        return lax.ppermute(block, "groups", [(i, i ^ mask) for i in range(groups)])

    wide = min(7, total)
    steps = range(tiles)

    straight = {step for step in steps if step % 4 == 2}
    counts = [5, 5] + [count for step in steps[1:] for count in ([5, 5] if step in straight else [wide])]

    def starts():
        found = [chip_start(total, 2), chip_start(total)]
        for step in steps[1:]:
            mask = TILE * step
            found += [chip_start(total, mask), chip_start(total, mask ^ 2)] if step in straight else [tile_start(total, step)]
        return found

    pieces = cuts(vol, starts, counts)
    span = -(-27 // groups)
    held = lax.dynamic_slice_in_dim(weight, jnp.minimum(group * span, 27 - span), span, 0)
    held, *pieces = lax.optimization_barrier((held, *pieces))
    far_own, own, *pieces = pieces
    held = jnp.stack([held] + [swap(held, TILE * step) for step in steps[1:]], axis=0)
    near, far, far_order = {0: own}, [], []
    for step in steps[1:]:
        if step in straight:
            near[step] = swap(after(pieces.pop(0), held), TILE * step)
            far.append(swap(after(pieces.pop(0), held), TILE * step ^ 2)[None])
            far_order.append([step])
        else:
            near[step] = swap(pieces.pop(0), TILE * step)
    far_held = swap(held, 2)
    columns = [jnp.stack([part] + [cross(part, mask) for mask in range(1, groups)], axis=0) for part in (held, far_held)]
    partner = chip_start(total, 2) - tile_start(total)
    for chosen in ([0, *steps[1::4]], [*steps[3::4]]):
        cut = [lax.dynamic_slice_in_dim(near[step], partner, 5, 0) if step else far_own for step in chosen]
        far.append(swap(jnp.stack(cut, axis=0), 2))
        far_order.append(chosen)
    kinds = tuple("chip" if step in straight or not step else "tile" for step in steps)
    near = [near[step] for step in steps]
    bias = jnp.broadcast_to(conv_bias[:, None], (weight.shape[2], vol.shape[3]))
    far[-2], bias = lax.optimization_barrier((far[-2], bias))
    taps = taps_of(tuple(steps), tuple(step for chosen in far_order for step in chosen), span, columns)
    parts = near + far
    shared = conv_call(send_body, total, kinds, parts, taps)
    came = swap(shared, 1)
    keep = conv_call(keep_body, total, kinds, parts, taps, shared, bias)
    out = upsample(keep, came, tconv_weight)
    return jnp.transpose(out, (0, 2, 1, 3))


def solution(mesh):
    return jax.shard_map(
        per_device,
        mesh=mesh,
        in_specs=(P("groups", "gx", None, None), P("gx", None, None), P(), P()),
        out_specs=P(("groups", "gx"), None, None, None),
        check_vma=False,
    )
```

```python
import functools

import jax
import jax.numpy as jnp
from jax import lax
from jax.experimental import pallas as pl
from jax.experimental.pallas import tpu as pltpu
from jax.sharding import PartitionSpec as P

TILE = 4
VMEM = pl.BlockSpec(memory_space=pltpu.VMEM)
PARTS = 3
PARAMS = pltpu.CompilerParams(vmem_limit_bytes=16 * 2**20)


def window(first, count, total):
    return jnp.clip(first, 0, total - count)


def chip_first():
    return lax.axis_index("gx") // 2 * 2


def tile_start(total, mask=0):
    return window(TILE * (lax.axis_index("gx") // TILE ^ mask) - 1, min(7, total), total)


def chip_start(total, mask=0):
    return window((chip_first() ^ mask) - 1, 5, total)


def after(value, *earlier):
    return lax.optimization_barrier((value, *earlier))[0]


def cut_body(starts, counts, vol_ref, *outs):
    for out_ref, start, count in zip(outs, starts(), counts):
        out_ref[...] = vol_ref[pl.ds(start, count)]


def cuts(vol, starts, counts):
    return pl.pallas_call(
        functools.partial(cut_body, starts, counts),
        out_shape=[jax.ShapeDtypeStruct((count, *vol.shape[1:]), vol.dtype) for count in counts],
        in_specs=[VMEM],
        out_specs=[VMEM] * len(counts),
        compiler_params=PARAMS,
    )(vol)


def taps_body(orders, span, *refs):
    weights, out_ref = refs[:-1], refs[-1]
    group = lax.axis_index("groups")
    cout = out_ref.shape[0] // 3
    for tap_z in range(3):
        pieces = []
        for tap in range(tap_z, 27, 3):
            part = tap // span
            start = min(part * span, 27 - span)
            for weight, order in zip(weights, orders):
                pieces += [weight[group ^ part, place, tap - start] for place in order]
        out_ref[tap_z * cout : (tap_z + 1) * cout] = jnp.concatenate(pieces, axis=0).T


def taps_of(orders, span, weights):
    cout, chans = weights[0].shape[-1], weights[0].shape[-2]
    columns = 9 * chans * sum(len(order) for order in orders)
    return pl.pallas_call(
        functools.partial(taps_body, orders, span),
        out_shape=jax.ShapeDtypeStruct((3 * cout, columns), jnp.bfloat16),
        in_specs=[VMEM] * len(weights),
        out_specs=VMEM,
        compiler_params=PARAMS,
        cost_estimate=pl.CostEstimate(flops=0, bytes_accessed=3 * 10**6, transcendentals=0),
    )(*weights)


def conv_planes(total, kinds, refs, taps, first, stores):
    steps = len(kinds)
    parts = [*refs[:steps], *(ref.at[at] for ref in refs[steps:] for at in range(ref.shape[0]))]
    kinds = [*kinds, *["chip"] * (len(parts) - steps)]
    _, wide_y, chans, wide_z = parts[0].shape
    cout = taps.shape[0] // 3
    lane = lax.broadcasted_iota(jnp.int32, (cout, wide_z), 1)
    zeros = jnp.zeros((len(parts) * chans, wide_z), taps.dtype)
    by_kind = {"tile": tile_start(total), "chip": chip_start(total)}
    starts = [by_kind[kind] for kind in kinds]
    rows = {(slot, y): zeros for slot in range(len(stores) + 2) for y in (-1, wide_y)}
    for slot in range(len(stores) + 2):
        at = first - 1 + slot
        inside = jnp.logical_and(at >= 0, at < total)
        index = [jnp.clip(at - starts[place], 0, ref.shape[0] - 1) for place, ref in enumerate(parts)]
        for y in range(wide_y):
            held = jnp.concatenate([ref[index[place], y] for place, ref in enumerate(parts)], axis=0)
            rows[slot, y] = jnp.where(inside, held, zeros)
    for plane, store in enumerate(stores):
        for pair in range(0, wide_y, 2):
            blocks = []
            for tap_x in range(3):
                for y in range(pair - 1, pair + 2):
                    blocks.append(jnp.concatenate([rows[plane + tap_x, y], rows[plane + tap_x, y + 1]], axis=1))
            acc = jnp.dot(taps[...], jnp.concatenate(blocks, axis=0), preferred_element_type=jnp.float32)
            for side in range(2):
                part = acc[:, side * wide_z : (side + 1) * wide_z]
                low = jnp.where(lane == 0, 0.0, pltpu.roll(part[:cout], 1, 1))
                high = jnp.where(lane == wide_z - 1, 0.0, pltpu.roll(part[2 * cout :], wide_z - 1, 1))
                store(pair + side, part[cout : 2 * cout] + low + high)


def early_body(total, kinds, *refs):
    *parts, taps, out_ref = refs
    core = lax.axis_index("gx") % 2

    def store_at(at):
        def store(y, value):
            out_ref[at, y] = value

        return store

    conv_planes(total, kinds, parts, taps, chip_first() + 1 - core, (store_at(core), store_at(1 - core)))
    conv_planes(total, kinds, parts, taps, chip_first() + 2 * core, (store_at(2),))


def send_body(total, kinds, *refs):
    *parts, taps, sums_ref, out_ref = refs
    core = lax.axis_index("gx") % 2

    def store_at(at):
        def store(y, value):
            out_ref[at, y] = sums_ref[at, y] + value

        return store

    conv_planes(total, kinds, parts, taps, chip_first() + 1 - core, (store_at(core), store_at(1 - core)))


def keep_body(total, kinds, *refs):
    *parts, taps, sums_ref, shared_ref, bias_ref, out_ref = refs
    core = lax.axis_index("gx") % 2
    bias = bias_ref[...]
    plane = chip_first() + 2 * core
    inside = plane < total

    def store(y, value):
        out_ref[core, y] = jnp.where(inside, sums_ref[2, y] + value + bias, -jnp.inf)
        out_ref[1 - core, y] = shared_ref[0, y] + bias

    conv_planes(total, kinds, parts, taps, plane, (store,))


def conv_call(body, planes, total, kinds, parts, taps, *more):
    _, wide_y, _, wide_z = parts[0].shape
    cout = taps.shape[0] // 3
    return pl.pallas_call(
        functools.partial(body, total, kinds),
        out_shape=jax.ShapeDtypeStruct((planes, wide_y, cout, wide_z), jnp.float32),
        in_specs=[VMEM] * (len(parts) + 1 + len(more)),
        out_specs=VMEM,
        compiler_params=PARAMS,
        cost_estimate=pl.CostEstimate(flops=10**7, bytes_accessed=10**5, transcendentals=0),
    )(*parts, taps, *more)


def up_body(keep_ref, came_ref, up_ref, out_ref, made, sems):
    core = lax.axis_index("gx") % 2
    _, wide_y, cout, wide_z = keep_ref.shape
    cup = up_ref.shape[1]
    hidden = []
    for ahead in range(2):
        at = jnp.where(core == ahead, 1, 0)
        rows = [jnp.maximum(keep_ref[ahead, y] + came_ref[at, y], 0.0).astype(jnp.bfloat16) for y in range(wide_y)]
        hidden.append(jnp.concatenate(rows, axis=1))
    shape = (2 * wide_z, 2 * wide_z)
    source, target = (lax.broadcasted_iota(jnp.int32, shape, axis) for axis in range(2))
    weave = (target == 2 * (source % wide_z) + source // wide_z).astype(jnp.bfloat16)
    edge = lax.broadcasted_iota(jnp.int32, (cup, wide_z), 1) == wide_z - 1

    def later(value):
        return jnp.where(edge, 0.0, pltpu.roll(value, wide_z - 1, 1))

    rest = [jnp.concatenate([value[:, wide_z:], jnp.zeros((cout, wide_z), value.dtype)], axis=1) for value in hidden]

    def taps(*firsts):
        return jnp.concatenate([up_ref[first : first + 3].reshape(3 * cup, cout) for first in firsts], axis=1)

    sides = (
        (taps(12), hidden[:1], taps(15, 9), [hidden[0], rest[0]]),
        (taps(21, 3), hidden, taps(24, 18, 6, 0), [hidden[0], rest[0], hidden[1], rest[1]]),
    )
    copies = []
    for odd, (left, right, left_odd, right_odd) in enumerate(sides):
        products = (
            jnp.dot(left, jnp.concatenate(right, axis=0), preferred_element_type=jnp.float32),
            jnp.dot(left_odd, jnp.concatenate(right_odd, axis=0), preferred_element_type=jnp.float32),
        )
        lines = []
        for y in range(wide_y):
            for product in products:
                moved, even, plain = (
                    product[tap * cup : (tap + 1) * cup, y * wide_z : (y + 1) * wide_z] for tap in range(3)
                )
                lines.append(jnp.concatenate([even, plain + later(moved)], axis=1).astype(jnp.bfloat16))
        share = len(lines) // PARTS
        for part in range(PARTS):
            rows = slice(part * share, (part + 1) * share)
            woven = jnp.dot(jnp.concatenate(lines[rows], axis=0), weave, preferred_element_type=jnp.float32)
            made[odd, rows] = woven.astype(jnp.bfloat16).reshape(share, cup, 2 * wide_z)
            copies.append(pltpu.make_async_copy(made.at[odd, rows], out_ref.at[odd, rows], sems.at[len(copies)]))
            copies[-1].start()
    for copy in copies:
        copy.wait()


def upsample(keep, came, up):
    _, wide_y, _, wide_z = keep.shape
    shape = (2, 2 * wide_y, up.shape[1], 2 * wide_z)
    return pl.pallas_call(
        up_body,
        out_shape=jax.ShapeDtypeStruct(shape, jnp.bfloat16),
        in_specs=[VMEM] * 3,
        out_specs=pl.BlockSpec(memory_space=pl.ANY),
        scratch_shapes=[pltpu.VMEM(shape, jnp.bfloat16), pltpu.SemaphoreType.DMA((2 * PARTS,))],
        compiler_params=PARAMS,
        cost_estimate=pl.CostEstimate(flops=10**9, bytes_accessed=3 * 10**6, transcendentals=0),
    )(keep, came, up)


def per_device(volume, conv_weight, conv_bias, tconv_weight):
    total, size, groups = volume.shape[0], lax.axis_size("gx"), lax.axis_size("groups")
    tiles = size // TILE
    assert total == size and size % TILE == 0 and tiles & (tiles - 1) == 0 and groups & (groups - 1) == 0
    group = lax.axis_index("groups")
    vol = jnp.transpose(volume, (0, 2, 1, 3))
    weight = jnp.transpose(conv_weight, (1, 0, 2))

    def swap(block, mask):
        return lax.ppermute(block, "gx", [(i, i ^ mask) for i in range(size)])

    def cross(block, mask):
        return lax.ppermute(block, "groups", [(i, i ^ mask) for i in range(groups)])

    wide = min(7, total)
    steps = range(tiles)

    straight = {step for step in steps if step % 4 == 2}
    counts = [5, 5] + [count for step in steps[1:] for count in ([5, 5] if step in straight else [wide])]

    def starts():
        found = [chip_start(total, 2), chip_start(total)]
        for step in steps[1:]:
            mask = TILE * step
            found += [chip_start(total, mask), chip_start(total, mask ^ 2)] if step in straight else [tile_start(total, step)]
        return found

    pieces = cuts(vol, starts, counts)
    span = -(-27 // groups)
    held = lax.dynamic_slice_in_dim(weight, jnp.minimum(group * span, 27 - span), span, 0)
    held, *pieces = lax.optimization_barrier((held, *pieces))
    far_own, own, *pieces = pieces
    held = jnp.stack([held] + [swap(held, TILE * step) for step in steps[1:]], axis=0)
    near, far, far_order = {0: own}, [], []
    for step in steps[1:]:
        if step in straight:
            near[step] = swap(after(pieces.pop(0), held), TILE * step)
            far.append(swap(after(pieces.pop(0), held), TILE * step ^ 2)[None])
            far_order.append([step])
        else:
            near[step] = swap(pieces.pop(0), TILE * step)
    far_held = swap(held, 2)
    columns = [jnp.stack([part] + [cross(part, mask) for mask in range(1, groups)], axis=0) for part in (held, far_held)]
    partner = chip_start(total, 2) - tile_start(total)
    for chosen in ([0, *steps[1::4]], [*steps[3::4]]):
        cut = [lax.dynamic_slice_in_dim(near[step], partner, 5, 0) if step else far_own for step in chosen]
        far.append(swap(jnp.stack(cut, axis=0), 2))
        far_order.append(chosen)
    bias = jnp.broadcast_to(conv_bias[:, None], (weight.shape[2], vol.shape[3]))
    far[-2], bias = lax.optimization_barrier((far[-2], bias))
    first = [step for step in steps if step not in straight]
    last = [step for step in steps if step in straight]
    taps = taps_of([tuple(first)], span, columns[:1])
    kinds = tuple("tile" if step else "chip" for step in first)
    sums = conv_call(early_body, 3, total, kinds, [near[step] for step in first], taps)
    taps = taps_of([tuple(last), tuple(step for chosen in far_order for step in chosen)], span, columns)
    kinds = ("chip",) * len(last)
    parts = [near[step] for step in last] + far
    shared = conv_call(send_body, 2, total, kinds, parts, taps, sums)
    came = swap(shared, 1)
    keep = conv_call(keep_body, 2, total, kinds, parts, taps, sums, shared, bias)
    out = upsample(keep, came, tconv_weight)
    return jnp.transpose(out, (0, 2, 1, 3))


def solution(mesh):
    return jax.shard_map(
        per_device,
        mesh=mesh,
        in_specs=(P("groups", "gx", None, None), P("gx", None, None), P(), P()),
        out_specs=P(("groups", "gx"), None, None, None),
        check_vma=False,
    )
```

```python
import functools

import jax
import jax.numpy as jnp
from jax import lax
from jax.experimental import pallas as pl
from jax.experimental.pallas import tpu as pltpu
from jax.sharding import PartitionSpec as P

TILE = 4
VMEM = pl.BlockSpec(memory_space=pltpu.VMEM)
PARTS = 3
PARAMS = pltpu.CompilerParams(vmem_limit_bytes=16 * 2**20)


def window(first, count, total):
    return jnp.clip(first, 0, total - count)


def chip_first():
    return lax.axis_index("gx") // 2 * 2


def tile_start(total, mask=0):
    return window(TILE * (lax.axis_index("gx") // TILE ^ mask) - 1, min(7, total), total)


def chip_start(total, mask=0):
    return window((chip_first() ^ mask) - 1, 5, total)


def after(value, *earlier):
    return lax.optimization_barrier((value, *earlier))[0]


def cut_body(starts, counts, vol_ref, *outs):
    for out_ref, start, count in zip(outs, starts(), counts):
        out_ref[...] = vol_ref[pl.ds(start, count)]


def cuts(vol, starts, counts):
    return pl.pallas_call(
        functools.partial(cut_body, starts, counts),
        out_shape=[jax.ShapeDtypeStruct((count, *vol.shape[1:]), vol.dtype) for count in counts],
        in_specs=[VMEM],
        out_specs=[VMEM] * len(counts),
        compiler_params=PARAMS,
    )(vol)


def taps_body(orders, span, *refs):
    weights, out_ref = refs[:-1], refs[-1]
    group = lax.axis_index("groups")
    cout = out_ref.shape[0] // 3
    for tap_z in range(3):
        pieces = []
        for tap in range(tap_z, 27, 3):
            part = tap // span
            start = min(part * span, 27 - span)
            for weight, order in zip(weights, orders):
                pieces += [weight[group ^ part, place, tap - start] for place in order]
        out_ref[tap_z * cout : (tap_z + 1) * cout] = jnp.concatenate(pieces, axis=0).T


def taps_of(orders, span, weights):
    cout, chans = weights[0].shape[-1], weights[0].shape[-2]
    columns = 9 * chans * sum(len(order) for order in orders)
    return pl.pallas_call(
        functools.partial(taps_body, orders, span),
        out_shape=jax.ShapeDtypeStruct((3 * cout, columns), jnp.bfloat16),
        in_specs=[VMEM] * len(weights),
        out_specs=VMEM,
        compiler_params=PARAMS,
        cost_estimate=pl.CostEstimate(flops=0, bytes_accessed=3 * 10**6, transcendentals=0),
    )(*weights)


def conv_planes(total, kinds, refs, taps, first, stores):
    steps = len(kinds)
    parts = [*refs[:steps], *(ref.at[at] for ref in refs[steps:] for at in range(ref.shape[0]))]
    kinds = [*kinds, *["chip"] * (len(parts) - steps)]
    _, wide_y, chans, wide_z = parts[0].shape
    cout = taps.shape[0] // 3
    lane = lax.broadcasted_iota(jnp.int32, (cout, wide_z), 1)
    zeros = jnp.zeros((len(parts) * chans, wide_z), taps.dtype)
    by_kind = {"tile": tile_start(total), "chip": chip_start(total)}
    starts = [by_kind[kind] for kind in kinds]
    rows = {(slot, y): zeros for slot in range(len(stores) + 2) for y in (-1, wide_y)}
    for slot in range(len(stores) + 2):
        at = first - 1 + slot
        inside = jnp.logical_and(at >= 0, at < total)
        index = [jnp.clip(at - starts[place], 0, ref.shape[0] - 1) for place, ref in enumerate(parts)]
        for y in range(wide_y):
            held = jnp.concatenate([ref[index[place], y] for place, ref in enumerate(parts)], axis=0)
            rows[slot, y] = jnp.where(inside, held, zeros)
    for plane, store in enumerate(stores):
        for pair in range(0, wide_y, 2):
            blocks = []
            for tap_x in range(3):
                for y in range(pair - 1, pair + 2):
                    blocks.append(jnp.concatenate([rows[plane + tap_x, y], rows[plane + tap_x, y + 1]], axis=1))
            acc = jnp.dot(taps[...], jnp.concatenate(blocks, axis=0), preferred_element_type=jnp.float32)
            for side in range(2):
                part = acc[:, side * wide_z : (side + 1) * wide_z]
                low = jnp.where(lane == 0, 0.0, pltpu.roll(part[:cout], 1, 1))
                high = jnp.where(lane == wide_z - 1, 0.0, pltpu.roll(part[2 * cout :], wide_z - 1, 1))
                store(pair + side, part[cout : 2 * cout] + low + high)


def early_body(total, kinds, *refs):
    *parts, taps, out_ref = refs
    core = lax.axis_index("gx") % 2

    def store_at(at):
        def store(y, value):
            out_ref[at, y] = value

        return store

    conv_planes(total, kinds, parts, taps, chip_first() + 1 - core, (store_at(core), store_at(1 - core)))
    conv_planes(total, kinds, parts, taps, chip_first() + 2 * core, (store_at(2),))


def send_body(total, kinds, *refs):
    *parts, taps, sums_ref, out_ref = refs
    core = lax.axis_index("gx") % 2

    def store_at(at):
        def store(y, value):
            out_ref[at, y] = sums_ref[at, y] + value

        return store

    conv_planes(total, kinds, parts, taps, chip_first() + 1 - core, (store_at(core), store_at(1 - core)))


def keep_body(total, kinds, *refs):
    *parts, taps, sums_ref, shared_ref, bias_ref, out_ref = refs
    core = lax.axis_index("gx") % 2
    bias = bias_ref[...]
    plane = chip_first() + 2 * core
    inside = plane < total

    def store(y, value):
        out_ref[core, y] = jnp.where(inside, sums_ref[2, y] + value + bias, -jnp.inf)
        out_ref[1 - core, y] = shared_ref[0, y] + bias

    conv_planes(total, kinds, parts, taps, plane, (store,))


def conv_call(body, planes, total, kinds, parts, taps, *more):
    _, wide_y, _, wide_z = parts[0].shape
    cout = taps.shape[0] // 3
    return pl.pallas_call(
        functools.partial(body, total, kinds),
        out_shape=jax.ShapeDtypeStruct((planes, wide_y, cout, wide_z), jnp.float32),
        in_specs=[VMEM] * (len(parts) + 1 + len(more)),
        out_specs=VMEM,
        compiler_params=PARAMS,
        cost_estimate=pl.CostEstimate(flops=10**7, bytes_accessed=10**5, transcendentals=0),
    )(*parts, taps, *more)


def up_body(keep_ref, came_ref, up_ref, out_ref, made, sems):
    core = lax.axis_index("gx") % 2
    _, wide_y, cout, wide_z = keep_ref.shape
    cup = up_ref.shape[1]
    hidden = []
    for ahead in range(2):
        at = jnp.where(core == ahead, 1, 0)
        rows = [jnp.maximum(keep_ref[ahead, y] + came_ref[at, y], 0.0).astype(jnp.bfloat16) for y in range(wide_y)]
        hidden.append(jnp.concatenate(rows, axis=1))
    shape = (2 * wide_z, 2 * wide_z)
    source, target = (lax.broadcasted_iota(jnp.int32, shape, axis) for axis in range(2))
    weave = (target == 2 * (source % wide_z) + source // wide_z).astype(jnp.bfloat16)
    edge = lax.broadcasted_iota(jnp.int32, (cup, wide_z), 1) == wide_z - 1

    def later(value):
        return jnp.where(edge, 0.0, pltpu.roll(value, wide_z - 1, 1))

    rest = [jnp.concatenate([value[:, wide_z:], jnp.zeros((cout, wide_z), value.dtype)], axis=1) for value in hidden]

    def taps(*firsts):
        return jnp.concatenate([up_ref[first : first + 3].reshape(3 * cup, cout) for first in firsts], axis=1)

    sides = (
        (taps(12), hidden[:1], taps(15, 9), [hidden[0], rest[0]]),
        (taps(21, 3), hidden, taps(24, 18, 6, 0), [hidden[0], rest[0], hidden[1], rest[1]]),
    )
    copies = []
    for odd, (left, right, left_odd, right_odd) in enumerate(sides):
        products = (
            jnp.dot(left, jnp.concatenate(right, axis=0), preferred_element_type=jnp.float32),
            jnp.dot(left_odd, jnp.concatenate(right_odd, axis=0), preferred_element_type=jnp.float32),
        )
        lines = []
        for y in range(wide_y):
            for product in products:
                moved, even, plain = (
                    product[tap * cup : (tap + 1) * cup, y * wide_z : (y + 1) * wide_z] for tap in range(3)
                )
                lines.append(jnp.concatenate([even, plain + later(moved)], axis=1).astype(jnp.bfloat16))
        share = len(lines) // PARTS
        for part in range(PARTS):
            rows = slice(part * share, (part + 1) * share)
            woven = jnp.dot(jnp.concatenate(lines[rows], axis=0), weave, preferred_element_type=jnp.float32)
            made[odd, rows] = woven.astype(jnp.bfloat16).reshape(share, cup, 2 * wide_z)
            copies.append(pltpu.make_async_copy(made.at[odd, rows], out_ref.at[odd, rows], sems.at[len(copies)]))
            copies[-1].start()
    for copy in copies:
        copy.wait()


def upsample(keep, came, up):
    _, wide_y, _, wide_z = keep.shape
    shape = (2, 2 * wide_y, up.shape[1], 2 * wide_z)
    return pl.pallas_call(
        up_body,
        out_shape=jax.ShapeDtypeStruct(shape, jnp.bfloat16),
        in_specs=[VMEM] * 3,
        out_specs=pl.BlockSpec(memory_space=pl.ANY),
        scratch_shapes=[pltpu.VMEM(shape, jnp.bfloat16), pltpu.SemaphoreType.DMA((2 * PARTS,))],
        compiler_params=PARAMS,
        cost_estimate=pl.CostEstimate(flops=10**9, bytes_accessed=3 * 10**6, transcendentals=0),
    )(keep, came, up)


def per_device(volume, conv_weight, conv_bias, tconv_weight):
    total, size, groups = volume.shape[0], lax.axis_size("gx"), lax.axis_size("groups")
    tiles = size // TILE
    assert total == size and size % TILE == 0 and tiles & (tiles - 1) == 0 and groups & (groups - 1) == 0
    group = lax.axis_index("groups")
    vol = jnp.transpose(volume, (0, 2, 1, 3))
    weight = jnp.transpose(conv_weight, (1, 0, 2))

    def swap(block, mask):
        return lax.ppermute(block, "gx", [(i, i ^ mask) for i in range(size)])

    def cross(block, mask):
        return lax.ppermute(block, "groups", [(i, i ^ mask) for i in range(groups)])

    wide = min(7, total)
    steps = range(tiles)

    straight = {step for step in steps if step % 4 == 2}
    counts = [5, 5] + [count for step in steps[1:] for count in ([5, 5] if step in straight else [wide])]

    def starts():
        found = [chip_start(total, 2), chip_start(total)]
        for step in steps[1:]:
            mask = TILE * step
            found += [chip_start(total, mask), chip_start(total, mask ^ 2)] if step in straight else [tile_start(total, step)]
        return found

    pieces = cuts(vol, starts, counts)
    span = -(-27 // groups)
    held = lax.dynamic_slice_in_dim(weight, jnp.minimum(group * span, 27 - span), span, 0)
    held, *pieces = lax.optimization_barrier((held, *pieces))
    far_own, own, *pieces = pieces
    held = jnp.stack([held] + [swap(held, TILE * step) for step in steps[1:]], axis=0)
    near, far, far_order = {0: own}, [], []
    for step in steps[1:]:
        if step in straight:
            near[step] = swap(after(pieces.pop(0), held), TILE * step)
            far.append(swap(pieces.pop(0), TILE * step ^ 2)[None])
            far_order.append([step])
        else:
            near[step] = swap(pieces.pop(0), TILE * step)
    far_held = swap(held, 2)
    columns = [jnp.stack([part] + [cross(part, mask) for mask in range(1, groups)], axis=0) for part in (held, far_held)]
    partner = chip_start(total, 2) - tile_start(total)
    for chosen in ([0, *steps[1::4]], [*steps[3::4]]):
        cut = [lax.dynamic_slice_in_dim(near[step], partner, 5, 0) if step else far_own for step in chosen]
        far.append(swap(jnp.stack(cut, axis=0), 2))
        far_order.append(chosen)
    bias = jnp.broadcast_to(conv_bias[:, None], (weight.shape[2], vol.shape[3]))
    far[-2], bias = lax.optimization_barrier((far[-2], bias))
    first = [step for step in steps if step not in straight]
    last = [step for step in steps if step in straight]
    taps = taps_of([tuple(first)], span, columns[:1])
    kinds = tuple("tile" if step else "chip" for step in first)
    sums = conv_call(early_body, 3, total, kinds, [near[step] for step in first], taps)
    taps = taps_of([tuple(last), tuple(step for chosen in far_order for step in chosen)], span, columns)
    kinds = ("chip",) * len(last)
    parts = [near[step] for step in last] + far
    shared = conv_call(send_body, 2, total, kinds, parts, taps, sums)
    came = swap(shared, 1)
    keep = conv_call(keep_body, 2, total, kinds, parts, taps, sums, shared, bias)
    out = upsample(keep, came, tconv_weight)
    return jnp.transpose(out, (0, 2, 1, 3))


def solution(mesh):
    return jax.shard_map(
        per_device,
        mesh=mesh,
        in_specs=(P("groups", "gx", None, None), P("gx", None, None), P(), P()),
        out_specs=P(("groups", "gx"), None, None, None),
        check_vma=False,
    )
```

```python
import functools

import jax
import jax.numpy as jnp
from jax import lax
from jax.experimental import pallas as pl
from jax.experimental.pallas import tpu as pltpu
from jax.sharding import PartitionSpec as P

TILE = 4
VMEM = pl.BlockSpec(memory_space=pltpu.VMEM)
PARTS = 3
PARAMS = pltpu.CompilerParams(vmem_limit_bytes=16 * 2**20)


def window(first, count, total):
    return jnp.clip(first, 0, total - count)


def chip_first():
    return lax.axis_index("gx") // 2 * 2


def tile_start(total, mask=0):
    return window(TILE * (lax.axis_index("gx") // TILE ^ mask) - 1, min(7, total), total)


def chip_start(total, mask=0):
    return window((chip_first() ^ mask) - 1, 5, total)


def after(value, *earlier):
    return lax.optimization_barrier((value, *earlier))[0]


def cut_body(starts, counts, vol_ref, *outs):
    for out_ref, start, count in zip(outs, starts(), counts):
        out_ref[...] = vol_ref[pl.ds(start, count)]


def cuts(vol, starts, counts):
    return pl.pallas_call(
        functools.partial(cut_body, starts, counts),
        out_shape=[jax.ShapeDtypeStruct((count, *vol.shape[1:]), vol.dtype) for count in counts],
        in_specs=[VMEM],
        out_specs=[VMEM] * len(counts),
        compiler_params=PARAMS,
    )(vol)


def taps_body(orders, span, *refs):
    weights, out_ref = refs[:-1], refs[-1]
    group = lax.axis_index("groups")
    cout = out_ref.shape[0] // 3
    for tap_z in range(3):
        pieces = []
        for tap in range(tap_z, 27, 3):
            part = tap // span
            start = min(part * span, 27 - span)
            for weight, order in zip(weights, orders):
                pieces += [weight[group ^ part, place, tap - start] for place in order]
        out_ref[tap_z * cout : (tap_z + 1) * cout] = jnp.concatenate(pieces, axis=0).T


def taps_of(orders, span, weights):
    cout, chans = weights[0].shape[-1], weights[0].shape[-2]
    columns = 9 * chans * sum(len(order) for order in orders)
    return pl.pallas_call(
        functools.partial(taps_body, orders, span),
        out_shape=jax.ShapeDtypeStruct((3 * cout, columns), jnp.bfloat16),
        in_specs=[VMEM] * len(weights),
        out_specs=VMEM,
        compiler_params=PARAMS,
        cost_estimate=pl.CostEstimate(flops=0, bytes_accessed=3 * 10**6, transcendentals=0),
    )(*weights)


def conv_planes(total, kinds, refs, taps, first, stores):
    steps = len(kinds)
    parts = [*refs[:steps], *(ref.at[at] for ref in refs[steps:] for at in range(ref.shape[0]))]
    kinds = [*kinds, *["chip"] * (len(parts) - steps)]
    _, wide_y, chans, wide_z = parts[0].shape
    cout = taps.shape[0] // 3
    lane = lax.broadcasted_iota(jnp.int32, (cout, wide_z), 1)
    zeros = jnp.zeros((len(parts) * chans, wide_z), taps.dtype)
    by_kind = {"tile": tile_start(total), "chip": chip_start(total)}
    starts = [by_kind[kind] for kind in kinds]
    rows = {(slot, y): zeros for slot in range(len(stores) + 2) for y in (-1, wide_y)}
    for slot in range(len(stores) + 2):
        at = first - 1 + slot
        inside = jnp.logical_and(at >= 0, at < total)
        index = [jnp.clip(at - starts[place], 0, ref.shape[0] - 1) for place, ref in enumerate(parts)]
        for y in range(wide_y):
            held = jnp.concatenate([ref[index[place], y] for place, ref in enumerate(parts)], axis=0)
            rows[slot, y] = jnp.where(inside, held, zeros)
    for plane, store in enumerate(stores):
        for pair in range(0, wide_y, 2):
            blocks = []
            for tap_x in range(3):
                for y in range(pair - 1, pair + 2):
                    blocks.append(jnp.concatenate([rows[plane + tap_x, y], rows[plane + tap_x, y + 1]], axis=1))
            acc = jnp.dot(taps[...], jnp.concatenate(blocks, axis=0), preferred_element_type=jnp.float32)
            for side in range(2):
                part = acc[:, side * wide_z : (side + 1) * wide_z]
                low = jnp.where(lane == 0, 0.0, pltpu.roll(part[:cout], 1, 1))
                high = jnp.where(lane == wide_z - 1, 0.0, pltpu.roll(part[2 * cout :], wide_z - 1, 1))
                store(pair + side, part[cout : 2 * cout] + low + high)


def early_body(total, kinds, *refs):
    *parts, taps, out_ref = refs
    core = lax.axis_index("gx") % 2

    def store_at(at):
        def store(y, value):
            out_ref[at, y] = value

        return store

    conv_planes(total, kinds, parts, taps, chip_first() + 1 - core, (store_at(core), store_at(1 - core)))
    conv_planes(total, kinds, parts, taps, chip_first() + 2 * core, (store_at(2),))


def send_body(total, kinds, *refs):
    *parts, taps, sums_ref, out_ref = refs
    core = lax.axis_index("gx") % 2

    def store_at(at):
        def store(y, value):
            out_ref[at, y] = sums_ref[at, y] + value

        return store

    conv_planes(total, kinds, parts, taps, chip_first() + 1 - core, (store_at(core), store_at(1 - core)))


def keep_body(total, kinds, *refs):
    *parts, taps, sums_ref, shared_ref, bias_ref, out_ref = refs
    core = lax.axis_index("gx") % 2
    bias = bias_ref[...]
    plane = chip_first() + 2 * core
    inside = plane < total

    def store(y, value):
        out_ref[core, y] = jnp.where(inside, sums_ref[2, y] + value + bias, -jnp.inf)
        out_ref[1 - core, y] = shared_ref[0, y] + bias

    conv_planes(total, kinds, parts, taps, plane, (store,))


def conv_call(body, planes, total, kinds, parts, taps, *more):
    _, wide_y, _, wide_z = parts[0].shape
    cout = taps.shape[0] // 3
    return pl.pallas_call(
        functools.partial(body, total, kinds),
        out_shape=jax.ShapeDtypeStruct((planes, wide_y, cout, wide_z), jnp.float32),
        in_specs=[VMEM] * (len(parts) + 1 + len(more)),
        out_specs=VMEM,
        compiler_params=PARAMS,
        cost_estimate=pl.CostEstimate(flops=10**6, bytes_accessed=10**4, transcendentals=0),
    )(*parts, taps, *more)


def up_body(keep_ref, came_ref, up_ref, out_ref, made, sems):
    core = lax.axis_index("gx") % 2
    _, wide_y, cout, wide_z = keep_ref.shape
    cup = up_ref.shape[1]
    hidden = []
    for ahead in range(2):
        at = jnp.where(core == ahead, 1, 0)
        rows = [jnp.maximum(keep_ref[ahead, y] + came_ref[at, y], 0.0).astype(jnp.bfloat16) for y in range(wide_y)]
        hidden.append(jnp.concatenate(rows, axis=1))
    shape = (2 * wide_z, 2 * wide_z)
    source, target = (lax.broadcasted_iota(jnp.int32, shape, axis) for axis in range(2))
    weave = (target == 2 * (source % wide_z) + source // wide_z).astype(jnp.bfloat16)
    edge = lax.broadcasted_iota(jnp.int32, (cup, wide_z), 1) == wide_z - 1

    def later(value):
        return jnp.where(edge, 0.0, pltpu.roll(value, wide_z - 1, 1))

    rest = [jnp.concatenate([value[:, wide_z:], jnp.zeros((cout, wide_z), value.dtype)], axis=1) for value in hidden]

    def taps(*firsts):
        return jnp.concatenate([up_ref[first : first + 3].reshape(3 * cup, cout) for first in firsts], axis=1)

    sides = (
        (taps(12), hidden[:1], taps(15, 9), [hidden[0], rest[0]]),
        (taps(21, 3), hidden, taps(24, 18, 6, 0), [hidden[0], rest[0], hidden[1], rest[1]]),
    )
    copies = []
    for odd, (left, right, left_odd, right_odd) in enumerate(sides):
        products = (
            jnp.dot(left, jnp.concatenate(right, axis=0), preferred_element_type=jnp.float32),
            jnp.dot(left_odd, jnp.concatenate(right_odd, axis=0), preferred_element_type=jnp.float32),
        )
        lines = []
        for y in range(wide_y):
            for product in products:
                moved, even, plain = (
                    product[tap * cup : (tap + 1) * cup, y * wide_z : (y + 1) * wide_z] for tap in range(3)
                )
                lines.append(jnp.concatenate([even, plain + later(moved)], axis=1).astype(jnp.bfloat16))
        share = len(lines) // PARTS
        for part in range(PARTS):
            rows = slice(part * share, (part + 1) * share)
            woven = jnp.dot(jnp.concatenate(lines[rows], axis=0), weave, preferred_element_type=jnp.float32)
            made[odd, rows] = woven.astype(jnp.bfloat16).reshape(share, cup, 2 * wide_z)
            copies.append(pltpu.make_async_copy(made.at[odd, rows], out_ref.at[odd, rows], sems.at[len(copies)]))
            copies[-1].start()
    for copy in copies:
        copy.wait()


def upsample(keep, came, up):
    _, wide_y, _, wide_z = keep.shape
    shape = (2, 2 * wide_y, up.shape[1], 2 * wide_z)
    return pl.pallas_call(
        up_body,
        out_shape=jax.ShapeDtypeStruct(shape, jnp.bfloat16),
        in_specs=[VMEM] * 3,
        out_specs=pl.BlockSpec(memory_space=pl.ANY),
        scratch_shapes=[pltpu.VMEM(shape, jnp.bfloat16), pltpu.SemaphoreType.DMA((2 * PARTS,))],
        compiler_params=PARAMS,
        cost_estimate=pl.CostEstimate(flops=10**9, bytes_accessed=3 * 10**6, transcendentals=0),
    )(keep, came, up)


def per_device(volume, conv_weight, conv_bias, tconv_weight):
    total, size, groups = volume.shape[0], lax.axis_size("gx"), lax.axis_size("groups")
    tiles = size // TILE
    assert total == size and size % TILE == 0 and tiles & (tiles - 1) == 0 and groups & (groups - 1) == 0
    group = lax.axis_index("groups")
    vol = jnp.transpose(volume, (0, 2, 1, 3))
    weight = jnp.transpose(conv_weight, (1, 0, 2))

    def swap(block, mask):
        return lax.ppermute(block, "gx", [(i, i ^ mask) for i in range(size)])

    def cross(block, mask):
        return lax.ppermute(block, "groups", [(i, i ^ mask) for i in range(groups)])

    wide = min(7, total)
    steps = range(tiles)

    straight = {step for step in steps if step % 4 == 2}
    counts = [5, 5] + [count for step in steps[1:] for count in ([5, 5] if step in straight else [wide])]

    def starts():
        found = [chip_start(total, 2), chip_start(total)]
        for step in steps[1:]:
            mask = TILE * step
            found += [chip_start(total, mask), chip_start(total, mask ^ 2)] if step in straight else [tile_start(total, step)]
        return found

    pieces = cuts(vol, starts, counts)
    span = -(-27 // groups)
    held = lax.dynamic_slice_in_dim(weight, jnp.minimum(group * span, 27 - span), span, 0)
    held, *pieces = lax.optimization_barrier((held, *pieces))
    far_own, own, *pieces = pieces
    held = jnp.stack([held] + [swap(held, TILE * step) for step in steps[1:]], axis=0)
    near, far, far_order = {0: own}, [], []
    for step in steps[1:]:
        if step in straight:
            near[step] = swap(after(pieces.pop(0), held), TILE * step)
            far.append(swap(pieces.pop(0), TILE * step ^ 2)[None])
            far_order.append([step])
        else:
            near[step] = swap(pieces.pop(0), TILE * step)
    far_held = swap(held, 2)
    columns = [jnp.stack([part] + [cross(part, mask) for mask in range(1, groups)], axis=0) for part in (held, far_held)]
    partner = chip_start(total, 2) - tile_start(total)
    for chosen in ([0, *steps[1::4]], [*steps[3::4]]):
        cut = [lax.dynamic_slice_in_dim(near[step], partner, 5, 0) if step else far_own for step in chosen]
        far.append(swap(jnp.stack(cut, axis=0), 2))
        far_order.append(chosen)
    bias = jnp.broadcast_to(conv_bias[:, None], (weight.shape[2], vol.shape[3]))
    far[-2], bias = lax.optimization_barrier((far[-2], bias))
    first = [step for step in steps if step not in straight]
    last = [step for step in steps if step in straight]
    taps = taps_of([tuple(first)], span, columns[:1])
    kinds = tuple("tile" if step else "chip" for step in first)
    sums = conv_call(early_body, 3, total, kinds, [near[step] for step in first], taps)
    taps = taps_of([tuple(last), tuple(step for chosen in far_order for step in chosen)], span, columns)
    kinds = ("chip",) * len(last)
    parts = [near[step] for step in last] + far
    shared = conv_call(send_body, 2, total, kinds, parts, taps, sums)
    came = swap(shared, 1)
    keep = conv_call(keep_body, 2, total, kinds, parts, taps, sums, shared, bias)
    out = upsample(keep, came, tconv_weight)
    return jnp.transpose(out, (0, 2, 1, 3))


def solution(mesh):
    return jax.shard_map(
        per_device,
        mesh=mesh,
        in_specs=(P("groups", "gx", None, None), P("gx", None, None), P(), P()),
        out_specs=P(("groups", "gx"), None, None, None),
        check_vma=False,
    )
```
